256 devices in a mesh: wide: 32 (over x, y, core), narrow: 8 (over z).
Axes of the slice: x: 4, y: 4, z: 8, core: 2. Of those that a mesh axis runs over, the one named last changes fastest.
Arguments:
- tokens: bfloat16 [2048, 7168], P(('wide', 'narrow')), may hold values from -6 to 6
- routes: int32 [2048, 8], P(('wide', 'narrow')), may hold values from 0 to 31, all different within a row; in each aligned block of 8 rows (0 to 7, 8 to 15, ...) at most 4 rows name the same one
- gates: float32 [2048, 8], P(('wide', 'narrow')), may hold values from 0.05 to 0.5
- fallback: int32 [32], replicated, may hold values from 0 to 31, each once
- w_gate: bfloat16 [32, 7168, 2048], P('wide', 'narrow'), may hold values from -0.0625 to 0.0625
- w_up: bfloat16 [32, 7168, 2048], P('wide', 'narrow'), may hold values from -0.0625 to 0.0625
- w_down: bfloat16 [32, 2048, 7168], P('wide', None, 'narrow'), may hold values from -0.125 to 0.125
Outputs:
- mixed: bfloat16 [2048, 7168], P(('wide', 'narrow'))
The draws below stay inside these ranges and needn't reach their ends.
Inputs may be any that keep to these rules, and one draw needn't show every extreme that they name: `routes`: each row names 8 different experts. Among the 8 rows of one device no expert is named more than 2 * 2 times, and in every draw some expert is named exactly 2 * 2 times by some device's rows. `fallback`: each expert appears once.
All inputs are finite; a program needn't handle non-finite values.
Results may differ from the reference program's by a relative error of at most 0.029.
Values may be sent and summed in bfloat16 or wider, within the bound.
A program may use at most 128 MiB of HBM per device.

```python
import math
import jax
import jax.numpy as jnp
import numpy as np
from jax import lax

D = 7168
FF = 2048
TOP = 8
TOK_DEV = 8
EXPERTS = 32
CAP = 2
TOKENS = 2048
N_NARROW = 8
DEVICES = 256


def block_scale(key, dims, split, least, largest):
    level, own = 1.0, jax.random.fold_in(key, 6)
    for axis_at, blocks in split:
        steps = jnp.exp(jax.random.uniform(jax.random.fold_in(own, axis_at), (blocks,), jnp.float32, least / len(split), largest / len(split)))
        level = level * jnp.repeat(steps, dims[axis_at] // blocks).reshape([-1 if axis == axis_at else 1 for axis in range(len(dims))])
    return level


def assign_block(rng, own, number, rows, count, top, bound, lean):
    ranking = jax.random.permutation(rng, count)
    heavy_load, usual = load_shares(count, rows * top, bound, lean, True), load_shares(count, rows * top, bound, lean, False)
    places = jnp.arange(count)

    def named(sizes, rotation):
        used = int((sizes > 0).sum())
        fixed = max(1, used // 4)
        passed = fixed + (places - fixed + rotation * (used - fixed)) % max(1, count - fixed)
        return jnp.zeros((count,), jnp.int32).at[ranking[jnp.where(places < fixed, places, passed)]].set(jnp.asarray(sizes, jnp.int32))

    sizes = jnp.where(number % 4 == 0, named(heavy_load, number // 4), named(usual, number - number // 4 - 1))
    mixed = jax.random.permutation(jax.random.fold_in(own, 3), count)
    donor, sink = mixed[0:count // 2 * 2:2], mixed[1:count // 2 * 2:2]
    slack = jnp.minimum(sizes[donor] - 1, bound - sizes[sink]) // 2
    slack = jnp.where((donor == ranking[0]) | (sink == ranking[0]) | (sizes[sink] == 0), 0, jnp.maximum(slack, 0))
    passed = jax.random.randint(jax.random.fold_in(own, 4), (count // 2,), 0, 1 << 20) % (slack + 1)
    sizes = sizes.at[donor].add(-passed).at[sink].add(passed)
    members = jnp.searchsorted(jnp.cumsum(sizes), jnp.arange(rows * top), side="right").astype(jnp.int32)
    grid = members.reshape(top, rows).T
    grid = grid[jax.random.permutation(jax.random.fold_in(own, 1), rows)]
    rotation = jax.random.randint(jax.random.fold_in(own, 2), (rows, 1), 0, top)
    return jnp.take_along_axis(grid, (jnp.arange(top)[None, :] + rotation) % top, axis=1)


def load_shares(number_of, total, reach, slope, full):
    weights = [(1 << 20) // math.isqrt(standing ** slope) + 1 for standing in range(1, number_of + 1)]
    largest = reach if full else min(reach, max(-(-total // number_of), total * weights[0] // sum(weights)))
    least = 1 if total - largest >= number_of - 1 else 0
    holding, rest = [largest] + [least] * (number_of - 1), total - largest - least * (number_of - 1)
    while rest > 0:
        free = [i for i in range(1, number_of) if holding[i] < largest] or [i for i in range(1, number_of) if holding[i] < reach]
        mass, budget = sum([weights[i] for i in free]), rest
        for i in free:
            more = min(reach - holding[i], max(1, budget * weights[i] // mass), rest)
            holding[i] = holding[i] + more
            rest = rest - more
    return np.array(holding)


def noise(rng, extent, width, most, pieces=(), held_as=jnp.bfloat16):
    loudness = block_scale(rng, extent, pieces, -0.22, 0.18) if pieces else 1.0
    drawn = jax.random.normal(rng, extent, jnp.float32) * width * loudness
    return jnp.minimum(jnp.maximum(drawn, -most), most).astype(held_as)


def setup_inputs(seed: int = 0) -> dict:
    arg_keys = jax.random.split(jax.random.key(seed), 8)
    tokens = noise(arg_keys[0], (TOKENS, D), 1.0, 6.0, ((0, 256),))
    routes_keys = jax.random.split(jax.random.fold_in(arg_keys[1], 1), TOKENS // TOK_DEV)
    routes_turns = jax.random.permutation(jax.random.fold_in(arg_keys[1], 3), TOKENS // TOK_DEV)
    routes = jax.vmap(lambda own, number: assign_block(jax.random.fold_in(arg_keys[1], 2), own, number, TOK_DEV, EXPERTS, TOP, 2 * CAP, 2))(routes_keys, routes_turns).reshape((TOKENS, TOP))
    gates = jnp.clip(jnp.exp(math.log(0.5) - 2.3025851 * jax.random.uniform(arg_keys[2], (TOKENS, TOP), jnp.float32) ** block_scale(arg_keys[2], (TOKENS, TOP), ((0, 256),), -0.2, 0.2)), 0.05, 0.5)
    fallback = jax.random.permutation(arg_keys[3], EXPERTS).astype(jnp.int32)
    w_gate = noise(arg_keys[4], (EXPERTS, D, FF), D ** -0.5, 0.0625, ((0, 32), (1, 8)))
    w_up = noise(arg_keys[5], (EXPERTS, D, FF), D ** -0.5, 0.0625, ((0, 32), (1, 8)))
    w_down = noise(arg_keys[6], (EXPERTS, FF, D), FF ** -0.5, 0.125, ((0, 32), (2, 8)))
    return dict(tokens=tokens, routes=routes, gates=gates, fallback=fallback, w_gate=w_gate, w_up=w_up, w_down=w_down)


def block_sums(rows, weight):
    block = D // N_NARROW
    parts = jnp.einsum("mnd,ndf->mnf", rows, weight.astype(jnp.float32).reshape(N_NARROW, block, FF), precision=lax.Precision.HIGHEST)
    rounded = lax.optimization_barrier(parts.astype(jnp.bfloat16))
    return jnp.sum(rounded.astype(jnp.float32), axis=1)


def reference(tokens, routes, gates, fallback, w_gate, w_up, w_down):
    most = DEVICES * 2 * CAP
    block = D // N_NARROW
    grouped = routes.reshape(DEVICES, TOK_DEV, TOP)
    onehot = (grouped[:, :, :, None] == jnp.arange(EXPERTS, dtype=jnp.int32)[None, None, None, :]).astype(jnp.int32)
    hits_all = jnp.sum(onehot, axis=2)
    before = jnp.cumsum(hits_all, axis=1) - hits_all
    rank = jnp.take_along_axis(before, grouped, axis=2).reshape(TOKENS, TOP)
    target = jnp.where(rank < CAP, routes, fallback[routes]).astype(jnp.int32)

    def one_expert(total, expert):
        hit = target == expert
        chosen = jnp.any(hit, axis=1)
        count = jnp.sum(chosen.astype(jnp.int32))
        index = jnp.nonzero(chosen, size=most, fill_value=0)[0].astype(jnp.int32)
        valid = jnp.arange(most, dtype=jnp.int32) < count
        rows = tokens[index].astype(jnp.float32).reshape(most, N_NARROW, block)
        gate = block_sums(rows, w_gate[expert])
        up_val = block_sums(rows, w_up[expert])
        hidden = (jax.nn.silu(gate) * up_val).astype(jnp.bfloat16)
        out_rows = jnp.dot(hidden, w_down[expert], preferred_element_type=jnp.float32).astype(jnp.bfloat16)
        weight = jnp.sum(jnp.where(hit[index], gates[index], 0.0), axis=1)
        weight = jnp.where(valid, weight, 0.0)
        total = total.at[index].add(weight[:, None] * out_rows.astype(jnp.float32))
        return total, None

    start = jnp.zeros((TOKENS, D), jnp.float32)
    total, _ = lax.scan(one_expert, start, jnp.arange(EXPERTS, dtype=jnp.int32))
    return total.astype(jnp.bfloat16)
```

```python
import functools

import jax
import jax.numpy as jnp
from jax import lax
from jax.experimental import pallas as pl
from jax.experimental.pallas import tpu as pltpu
from jax.sharding import PartitionSpec as P

F32 = jnp.float32
BF16 = jnp.bfloat16
NX, NY, NC, NZ = 4, 4, 2, 8
SIDE = 128
WIDE_LO = 512
SUBS = 4


def dot(a, b):
    return jnp.dot(a, b, preferred_element_type=F32)


class Copies:
    def __init__(self, send, recv):
        self.send, self.recv = send, recv
        self.used = 0
        self.started = []

    def slot(self):
        self.used += 1
        return self.used - 1

    def make(self, slot, src, dst, device):
        return pltpu.make_async_remote_copy(
            src_ref=src,
            dst_ref=dst,
            send_sem=self.send.at[slot],
            recv_sem=self.recv.at[slot],
            device_id=device,
            device_id_type=pl.DeviceIdType.MESH,
        )

    def go(self, slot, src, dst, device):
        copy = self.make(slot, src, dst, device)
        copy.start()
        self.started.append(copy)


def kernel(
    tok,
    wg_hbm,
    wu_hbm,
    wd_hbm,
    out,
    zin,
    g,
    x,
    sel,
    wcol,
    wg,
    wu,
    wd,
    first,
    part,
    hid,
    acc,
    c,
    core_in,
    ra1,
    ra2,
    rb1,
    rb2,
    zout,
    zback,
    load_sem,
    send,
    recv,
    rs_send,
    rs_recv,
    ag_send,
    ag_recv,
):
    wide, z = lax.axis_index("wide"), lax.axis_index("narrow")
    cc = lax.rem(wide, NC)
    yy = lax.rem(wide // NC, NY)
    xx = wide // (NC * NY)
    block = x.shape[1]
    rows = x.shape[0]
    half = rows // 2
    sub = half // SUBS
    cols = wg.shape[1] // NZ

    def at(px, py, pc):
        return (px * NY + py) * NC + pc

    def xs(k):
        return lax.rem(xx + k, NX)

    def ys(k):
        return lax.rem(yy + k, NY)

    def zs(k):
        return lax.rem(z + k, NZ)

    xdev = {1: (at(xs(1), yy, cc), z), -1: (at(xs(3), yy, cc), z)}
    ydev = {1: (at(xx, ys(1), cc), z), -1: (at(xx, ys(3), cc), z)}
    mate = (at(xx, yy, 1 - cc), z)

    loads = [
        pltpu.make_async_copy(a, b, load_sem.at[i])
        for i, (a, b) in enumerate(((wg_hbm, wg), (wu_hbm, wu), (wd_hbm, wd)))
    ]
    for load in loads:
        load.start()

    barrier = pltpu.get_barrier_semaphore()
    peers = [xdev[1], xdev[-1], ydev[1], ydev[-1], mate] + [(wide, zs(k)) for k in range(1, NZ)]
    for peer in peers:
        pl.semaphore_signal(barrier, inc=1, device_id=peer, device_id_type=pl.DeviceIdType.MESH)
    pl.semaphore_wait(barrier, len(peers))

    copies = Copies(send, recv)

    zslots = {}
    for k in range(1, NZ):
        zslots[k] = copies.slot()
        copies.go(zslots[k], tok.at[zs(k)], zin.at[z], (wide, zs(k)))
    zin[z] = tok[z]
    for k in range(1, NZ):
        src = zs(NZ - k)
        copies.make(zslots[k], tok.at[src], zin.at[src], (wide, src)).wait_recv()
    arrived = zin[...].astype(F32)
    tokens_z = arrived.shape[0] * arrived.shape[1] // 2
    g[xx, yy, cc, :, :WIDE_LO] = arrived[:, :8, :].reshape(tokens_z, WIDE_LO).astype(BF16)
    g[xx, yy, cc, :, WIDE_LO:] = arrived[:, 8:, :].reshape(tokens_z, WIDE_LO).astype(BF16)

    def lane_a(pos):
        return lambda lo, n: g.at[pos, yy, cc, pl.ds(lo, n)]

    def lane_b(pos):
        return lambda lo, n: g.at[xx, pos, cc, pl.ds(32 + lo, n)]

    def plane_a(pos):
        return lambda lo, n: g.at[:, pos, cc, pl.ds(lo, n)]

    def plane_b(pos):
        return lambda lo, n: g.at[pos, :, cc, pl.ds(32 + lo, n)]

    def gather_start(region, step, dev):
        right, left = copies.slot(), copies.slot()
        own = region(step(0))(0, 32)
        copies.go(right, own, own, dev[1])
        copies.go(left, own, own, dev[-1])
        return right, left

    def gather_forward(region, step, dev, slots):
        right, left = copies.slot(), copies.slot()
        before, after = region(step(3)), region(step(1))
        copies.make(slots[0], before(0, 32), before(0, 32), dev[-1]).wait_recv()
        copies.go(right, before(0, 16), before(0, 16), dev[1])
        copies.make(slots[1], after(0, 32), after(0, 32), dev[1]).wait_recv()
        copies.go(left, after(16, 16), after(16, 16), dev[-1])
        return right, left

    def gather_end(region, step, dev, slots):
        far = region(step(2))
        copies.make(slots[0], far(0, 16), far(0, 16), dev[-1]).wait_recv()
        copies.make(slots[1], far(16, 16), far(16, 16), dev[1]).wait_recv()

    core_waits = []

    def to_mate(region, step, k):
        slot = copies.slot()
        copies.go(slot, region(step(k))(0, 32), region(step(k))(0, 32), mate)
        core_waits.append((slot, region, step, k))

    a1 = gather_start(lane_a, xs, xdev)
    b1 = gather_start(lane_b, ys, ydev)
    a2 = gather_forward(lane_a, xs, xdev, a1)
    b2 = gather_forward(lane_b, ys, ydev, b1)
    gather_end(lane_a, xs, xdev, a2)
    a3 = gather_start(plane_a, ys, ydev)
    gather_end(lane_b, ys, ydev, b2)
    b3 = gather_start(plane_b, xs, xdev)
    to_mate(plane_a, ys, 0)
    to_mate(plane_b, xs, 0)
    a4 = gather_forward(plane_a, ys, ydev, a3)
    b4 = gather_forward(plane_b, xs, xdev, b3)
    for k in (1, 3):
        to_mate(plane_a, ys, k)
        to_mate(plane_b, xs, k)
    gather_end(plane_a, ys, ydev, a4)
    to_mate(plane_a, ys, 2)
    gather_end(plane_b, xs, xdev, b4)
    to_mate(plane_b, xs, 2)
    other = {
        plane_a: lambda pos: g.at[:, pos, 1 - cc, pl.ds(0, 32)],
        plane_b: lambda pos: g.at[pos, :, 1 - cc, pl.ds(32, 32)],
    }
    for slot, region, step, k in core_waits:
        there = other[region](step(k))
        copies.make(slot, there, there, mate).wait_recv()

    batches = 8
    toks = NX * NY * NC * 64 // batches
    slots = rows // batches
    devs = slots // 4
    lane = lax.broadcasted_iota(jnp.int32, (toks, SIDE), 1)
    row = lax.broadcasted_iota(jnp.int32, (toks, SIDE), 0)
    mine = (lax.rem(lane, 32) == wide) & (lane < 96)
    square_r = lax.broadcasted_iota(jnp.int32, (toks, toks), 0)
    square_c = lax.broadcasted_iota(jnp.int32, (toks, toks), 1)
    lower = ((square_r // 8 == square_c // 8) & (square_c < square_r)).astype(F32).astype(BF16)
    for b in range(batches):
        here = g[b // 2, 2 * (b % 2) : 2 * (b % 2) + 2].reshape(toks, block + SIDE)
        weight = jnp.sum(
            jnp.where(mine, here[:, block:].astype(F32), 0.0), axis=1, keepdims=True
        )
        weight = jnp.broadcast_to(weight, (toks, SIDE))
        chosen = jnp.where(weight > 0.0, 1.0, 0.0)
        rank = dot(lower, chosen.astype(BF16)).astype(jnp.int32)
        place = rank * devs + row // 8
        pick = jnp.where((lane == place) & (weight > 0.0), 1.0, 0.0).astype(BF16)
        sel[b] = pick
        wcol[b] = weight
        taken = lax.dot_general(
            pick, here[:, :block], (((0,), (0,)), ((), ())), preferred_element_type=F32
        )
        x[b * slots : (b + 1) * slots, :] = taken.astype(BF16)

    loads[0].wait()
    loads[1].wait()
    zdev = ((wide, zs(1)), (wide, zs(NZ - 1)))

    def ring(s, d):
        return lax.rem(z + NZ - s, NZ) if d == 0 else lax.rem(z + s, NZ)

    def product(d, q, chunk):
        rows_here = x[pl.ds(pl.multiple_of(d * half + q * sub, sub), sub), :]
        at_cols = pl.ds(pl.multiple_of(chunk * cols, cols), cols)
        return dot(rows_here, wg[:, at_cols]), dot(rows_here, wu[:, at_cols])

    def rs_copy(d, s, q, src):
        return pltpu.make_async_remote_copy(
            src_ref=src,
            dst_ref=part.at[d, s, q],
            send_sem=rs_send.at[d, s, q],
            recv_sem=rs_recv.at[d, s, q],
            device_id=zdev[d],
            device_id_type=pl.DeviceIdType.MESH,
        )

    def ag_copy(d, s, q, chunk):
        here = hid.at[chunk, pl.ds(pl.multiple_of(d * half + q * sub, sub), sub)]
        return pltpu.make_async_remote_copy(
            src_ref=here,
            dst_ref=here,
            send_sem=ag_send.at[d, s, q],
            recv_sem=ag_recv.at[d, s, q],
            device_id=zdev[d],
            device_id_type=pl.DeviceIdType.MESH,
        )

    def each_sub(body):
        def step(q, carry):
            for d in range(2):
                body(d, q)
            return carry

        lax.fori_loop(0, SUBS, step, 0)

    def rs_first(d, q):
        gate, up = product(d, q, ring(1, d))
        first[d, q, :, :cols] = gate.astype(BF16)
        first[d, q, :, cols:] = up.astype(BF16)
        rs_copy(d, 0, q, first.at[d, q]).start()

    each_sub(rs_first)

    def rs_step(s, carry):
        def body(d, q):
            gate, up = product(d, q, ring(s + 1, d))
            rs_copy(d, s - 1, q, first.at[d, q]).wait_recv()
            here = part.at[d, s - 1, q]
            here[:, :cols] = (here[:, :cols].astype(F32) + gate).astype(BF16)
            here[:, cols:] = (here[:, cols:].astype(F32) + up).astype(BF16)
            rs_copy(d, s, q, here).start()

        each_sub(body)
        return carry

    lax.fori_loop(1, NZ - 1, rs_step, 0)
    loads[2].wait()

    def down(d, q, chunk):
        at_rows = pl.ds(pl.multiple_of(d * half + q * sub, sub), sub)
        at_cols = pl.ds(pl.multiple_of(chunk * cols, cols), cols)
        return at_rows, dot(hid[chunk, at_rows, :], wd[at_cols, :])

    def rs_last(d, q):
        gate, up = product(d, q, z)
        rs_copy(d, NZ - 2, q, first.at[d, q]).wait_recv()
        here = part.at[d, NZ - 2, q]
        gate = gate + here[:, :cols].astype(F32)
        up = up + here[:, cols:].astype(F32)
        hidden = gate / (1.0 + jnp.exp(-gate)) * up
        at_rows = pl.ds(pl.multiple_of(d * half + q * sub, sub), sub)
        hid[z, at_rows, :] = hidden.astype(BF16)
        ag_copy(d, 0, q, z).start()
        at_rows, value = down(d, q, z)
        acc[at_rows, :] = value

    each_sub(rs_last)

    def ag_step(s, carry):
        def body(d, q):
            chunk = ring(s, d)
            ag_copy(d, s - 1, q, chunk).wait_recv()
            ag_copy(d, s, q, chunk).start()
            at_rows, value = down(d, q, chunk)
            acc[at_rows, :] = acc[at_rows, :] + value

        each_sub(body)
        return carry

    lax.fori_loop(1, NZ - 1, ag_step, 0)

    core_slots = [copies.slot() for _ in range(NX)]
    for b in range(batches):
        d, q = b // SUBS, b % SUBS
        chunk = ring(NZ - 1, d)
        ag_copy(d, NZ - 2, q, chunk).wait_recv()
        at_rows, value = down(d, q, chunk)
        expert_out = (acc[at_rows, :] + value).astype(BF16)
        mixed = dot(sel[b], expert_out) * wcol[b][:, :1]
        c[b // 2, 2 * (b % 2) : 2 * (b % 2) + 2] = mixed.astype(BF16).reshape(2, NC, 64, block)
        if b % 2 == 1:
            copies.go(core_slots[b // 2], c.at[b // 2, :, 1 - cc], core_in.at[b // 2], mate)
    for px in range(NX):
        copies.make(core_slots[px], c.at[px, :, cc], core_in.at[px], mate).wait_recv()
        c[px, :, cc] = (c[px, :, cc].astype(F32) + core_in[px].astype(F32)).astype(BF16)

    def c_plane_a(pos, lo, n):
        return c.at[:, pos, cc, pl.ds(lo, n)]

    def c_plane_b(pos, lo, n):
        return c.at[pos, :, cc, pl.ds(32 + lo, n)]

    def c_lane_a(pos, lo, n):
        return c.at[pos, yy, cc, pl.ds(lo, n)]

    def c_lane_b(pos, lo, n):
        return c.at[xx, pos, cc, pl.ds(32 + lo, n)]

    def add_into(ref, other_ref):
        ref[...] = (ref[...].astype(F32) + other_ref[...].astype(F32)).astype(BF16)

    def scatter_start(region, step, dev, buf):
        right, left = copies.slot(), copies.slot()
        copies.go(right, region(step(2), 0, 16), buf.at[0], dev[1])
        copies.go(left, region(step(2), 16, 16), buf.at[1], dev[-1])
        return right, left

    def scatter_forward(region, step, dev, buf, buf2, slots):
        right, left = copies.slot(), copies.slot()
        copies.make(slots[0], region(step(2), 0, 16), buf.at[0], dev[-1]).wait_recv()
        add_into(region(step(1), 0, 16), buf.at[0])
        copies.go(right, region(step(1), 0, 32), buf2.at[0], dev[1])
        copies.make(slots[1], region(step(2), 16, 16), buf.at[1], dev[1]).wait_recv()
        add_into(region(step(3), 16, 16), buf.at[1])
        copies.go(left, region(step(3), 0, 32), buf2.at[1], dev[-1])
        return right, left

    def scatter_end(region, step, dev, buf2, slots):
        copies.make(slots[0], region(step(0), 0, 32), buf2.at[0], dev[-1]).wait_recv()
        copies.make(slots[1], region(step(0), 0, 32), buf2.at[1], dev[1]).wait_recv()
        here = region(step(0), 0, 32)
        return here[...].astype(F32) + buf2[0].astype(F32) + buf2[1].astype(F32)

    a1 = scatter_start(c_plane_a, ys, ydev, ra1.at[0])
    b1 = scatter_start(c_plane_b, xs, xdev, ra1.at[1])
    a2 = scatter_forward(c_plane_a, ys, ydev, ra1.at[0], ra2.at[0], a1)
    b2 = scatter_forward(c_plane_b, xs, xdev, ra1.at[1], ra2.at[1], b1)
    total = scatter_end(c_plane_a, ys, ydev, ra2.at[0], a2)
    c[:, yy, cc, :32, :] = total.astype(BF16)
    a3 = scatter_start(c_lane_a, xs, xdev, rb1.at[0])
    total = scatter_end(c_plane_b, xs, xdev, ra2.at[1], b2)
    c[xx, :, cc, 32:, :] = total.astype(BF16)
    b3 = scatter_start(c_lane_b, ys, ydev, rb1.at[1])
    a4 = scatter_forward(c_lane_a, xs, xdev, rb1.at[0], rb2.at[0], a3)
    b4 = scatter_forward(c_lane_b, ys, ydev, rb1.at[1], rb2.at[1], b3)
    sums = [
        scatter_end(c_lane_a, xs, xdev, rb2.at[0], a4),
        scatter_end(c_lane_b, ys, ydev, rb2.at[1], b4),
    ]

    for i, total in enumerate(sums):
        lo = total[:, :WIDE_LO].reshape(4, 8, WIDE_LO)
        hi = total[:, WIDE_LO:].reshape(4, 8, block - WIDE_LO)
        hi = jnp.concatenate([hi, jnp.zeros((4, 8, 2 * WIDE_LO - block), F32)], axis=2)
        zout[4 * i : 4 * i + 4] = jnp.concatenate([lo, hi], axis=1).astype(BF16)
    zslots = {}
    for k in range(1, NZ):
        zslots[k] = copies.slot()
        copies.go(zslots[k], zout.at[zs(k)], zback.at[z], (wide, zs(k)))
    zback[z] = zout[z]
    for k in range(1, NZ):
        src = zs(NZ - k)
        copies.make(zslots[k], zout.at[src], zback.at[src], (wide, src)).wait_recv()
    pieces = []
    for n in range(NZ):
        got = zback[n].astype(F32)
        pieces += [got[:8, :], got[8:, : block - WIDE_LO]]
    out[...] = jnp.concatenate(pieces, axis=1).astype(BF16)

    for copy in copies.started:
        copy.wait_send()

    def drain(s, carry):
        def body(d, q):
            rs_copy(d, s, q, first.at[d, q]).wait_send()
            ag_copy(d, s, q, ring(s, d)).wait_send()

        each_sub(body)
        return carry

    lax.fori_loop(0, NZ - 1, drain, 0)


def on_device(tokens, routes, gates, fallback, w_gate, w_up, w_down):
    experts = lax.axis_size("wide")
    narrow = lax.axis_size("narrow")
    tok_rows, width = tokens.shape
    block = width // narrow
    ff = w_gate.shape[2]
    capacity = min(tok_rows // 2, tok_rows * routes.shape[1] // experts)
    rows = experts * narrow * 2 * capacity
    half = rows // 2
    sub = half // SUBS
    cols = ff // narrow

    expert_ids = jnp.arange(experts, dtype=jnp.int32)
    matched = routes[:, :, None] == expert_ids[None, None, :]
    hits = jnp.sum(matched.astype(jnp.int32), axis=1)
    weight_of = jnp.sum(jnp.where(matched, gates[:, :, None], 0.0), axis=1)
    ranks = jnp.cumsum(hits, axis=0) - hits
    primary = jnp.where(ranks < capacity, weight_of, 0.0)
    overflow = jnp.where(ranks < capacity, 0.0, weight_of)
    redirect = fallback[:, None] == expert_ids[None, :]
    weights = primary + jnp.sum(jnp.where(redirect[None], overflow[:, :, None], 0.0), axis=1)
    high = lax.reduce_precision(weights, 8, 7)
    middle = lax.reduce_precision(weights - high, 8, 7)
    low = weights - high - middle
    side = jnp.concatenate([high, middle, low, jnp.zeros_like(low)], axis=1).astype(BF16)
    pieces = tokens.reshape(tok_rows, narrow, block).transpose(1, 0, 2)
    side = jnp.broadcast_to(side[None], (narrow, tok_rows, SIDE))
    tok = jnp.concatenate(
        [pieces[:, :, :WIDE_LO], jnp.concatenate([pieces[:, :, WIDE_LO:], side], axis=2)], axis=1
    )

    vmem = pl.BlockSpec(memory_space=pltpu.VMEM)
    hbm = pl.BlockSpec(memory_space=pl.ANY)
    line = block + SIDE
    copies = 7 + 24 + 4 + 16 + 7
    return pl.pallas_call(
        kernel,
        out_shape=jax.ShapeDtypeStruct((tok_rows, width), BF16),
        in_specs=[vmem, hbm, hbm, hbm],
        out_specs=vmem,
        scratch_shapes=[
            pltpu.VMEM((NZ, 16, WIDE_LO), BF16),
            pltpu.VMEM((NX, NY, NC, 64, line), BF16),
            pltpu.VMEM((rows, block), BF16),
            pltpu.VMEM((8, 256, SIDE), BF16),
            pltpu.VMEM((8, 256, SIDE), F32),
            pltpu.VMEM((block, ff), BF16),
            pltpu.VMEM((block, ff), BF16),
            pltpu.VMEM((ff, block), BF16),
            pltpu.VMEM((2, SUBS, sub, 2 * cols), BF16),
            pltpu.VMEM((2, NZ - 1, SUBS, sub, 2 * cols), BF16),
            pltpu.VMEM((NZ, rows, cols), BF16),
            pltpu.VMEM((rows, block), F32),
            pltpu.VMEM((NX, NY, NC, 64, block), BF16),
            pltpu.VMEM((NX, NY, 64, block), BF16),
            pltpu.VMEM((2, 2, 4, 16, block), BF16),
            pltpu.VMEM((2, 2, 4, 32, block), BF16),
            pltpu.VMEM((2, 2, 16, block), BF16),
            pltpu.VMEM((2, 2, 32, block), BF16),
            pltpu.VMEM((NZ, 16, WIDE_LO), BF16),
            pltpu.VMEM((NZ, 16, WIDE_LO), BF16),
            pltpu.SemaphoreType.DMA((3,)),
            pltpu.SemaphoreType.DMA((copies,)),
            pltpu.SemaphoreType.DMA((copies,)),
            pltpu.SemaphoreType.DMA((2, NZ - 1, SUBS)),
            pltpu.SemaphoreType.DMA((2, NZ - 1, SUBS)),
            pltpu.SemaphoreType.DMA((2, NZ - 1, SUBS)),
            pltpu.SemaphoreType.DMA((2, NZ - 1, SUBS)),
        ],
        compiler_params=pltpu.CompilerParams(
            collective_id=0, has_side_effects=True, vmem_limit_bytes=58 * 1024 * 1024
        ),
        cost_estimate=pl.CostEstimate(
            flops=6 * rows * block * ff, bytes_accessed=6 * block * ff, transcendentals=rows * cols
        ),
        name="experts",
    )(tok, w_gate[0], w_up[0], w_down[0])


def solution(mesh):
    placed = (
        P(("wide", "narrow"), None),
        P(("wide", "narrow"), None),
        P(("wide", "narrow"), None),
        P(),
        P("wide", "narrow", None),
        P("wide", "narrow", None),
        P("wide", None, "narrow"),
    )
    return jax.shard_map(
        on_device,
        mesh=mesh,
        in_specs=placed,
        out_specs=P(("wide", "narrow"), None),
        check_vma=False,
    )
```

```python
import functools

import jax
import jax.numpy as jnp
from jax import lax
from jax.experimental import pallas as pl
from jax.experimental.pallas import tpu as pltpu
from jax.sharding import PartitionSpec as P

F32 = jnp.float32
BF16 = jnp.bfloat16
NX, NY, NC, NZ = 4, 4, 2, 8
SIDE = 128
WIDE_LO = 512
GROUPS = 4


def dot(a, b):
    return jnp.dot(a, b, preferred_element_type=F32)


def kernel(
    tok,
    wg_hbm,
    wu_hbm,
    wd_hbm,
    out,
    zin,
    g,
    x,
    sel,
    wcol,
    wg,
    wu,
    wd,
    first,
    part,
    hid,
    acc,
    c,
    core_in,
    land,
    zout,
    zback,
    load_sem,
    z_send,
    z_recv,
    g_send,
    g_recv,
    m_send,
    m_recv,
    rs_send,
    rs_recv,
    ag_send,
    ag_recv,
    cm_send,
    cm_recv,
    r_send,
    r_recv,
    b_send,
    b_recv,
):
    wide, z = lax.axis_index("wide"), lax.axis_index("narrow")
    cc = lax.rem(wide, NC)
    yy = lax.rem(wide // NC, NY)
    xx = wide // (NC * NY)
    block = x.shape[3]
    cols = wg.shape[1] // NZ
    side = g.shape[4] - block

    def at(px, py, pc):
        return (px * NY + py) * NC + pc

    def zs(k):
        return lax.rem(z + k, NZ)

    def chip(k):
        return lax.rem(xx + k // NY, NX), lax.rem(yy + lax.rem(k, NY), NY)

    def chip_back(k):
        return lax.rem(xx + NX - k // NY, NX), lax.rem(yy + NY - lax.rem(k, NY), NY)

    mate = (at(xx, yy, 1 - cc), z)

    def remote(src, dst, send, recv, device):
        return pltpu.make_async_remote_copy(
            src_ref=src,
            dst_ref=dst,
            send_sem=send,
            recv_sem=recv,
            device_id=device,
            device_id_type=pl.DeviceIdType.MESH,
        )

    def loop(lo, hi, body):
        def step(i, carry):
            body(i)
            return carry

        lax.fori_loop(lo, hi, step, 0)

    loads = [
        pltpu.make_async_copy(a, b, load_sem.at[i])
        for i, (a, b) in enumerate(((wg_hbm, wg), (wu_hbm, wu), (wd_hbm, wd)))
    ]
    for load in loads:
        load.start()

    barrier = pltpu.get_barrier_semaphore()

    def greet(device):
        pl.semaphore_signal(barrier, inc=1, device_id=device, device_id_type=pl.DeviceIdType.MESH)

    for k in range(1, NZ):
        greet((wide, zs(k)))
    greet(mate)
    loop(1, NX * NY, lambda k: greet((at(*chip(k), cc), z)))
    pl.semaphore_wait(barrier, NZ - 1 + 1 + NX * NY - 1)

    def z_copy(to):
        return remote(tok.at[to], zin.at[z], z_send.at[to], z_recv.at[z], (wide, to))

    def z_from(src):
        return remote(tok.at[src], zin.at[src], z_send.at[src], z_recv.at[src], (wide, src))

    loop(1, NZ, lambda k: z_copy(zs(k)).start())
    zin[z] = tok[z]

    def group_rows(h):
        return pl.ds(16 * h, 16)

    def g_copy(h, k):
        px, py = chip(k)
        here = g.at[xx, yy, cc, group_rows(h)]
        return remote(here, here, g_send.at[h, k], g_recv.at[h, k], (at(px, py, cc), z))

    def g_from(h, k):
        px, py = chip_back(k)
        there = g.at[px, py, cc, group_rows(h)]
        return remote(there, there, g_send.at[h, k], g_recv.at[h, k], (at(px, py, cc), z))

    def prepare(h):
        for src in (2 * h, 2 * h + 1):
            pl.when(z != src)(lambda src=src: z_from(src).wait_recv())
        arrived = zin[2 * h : 2 * h + 2].astype(F32)
        for half in range(2):
            lanes = slice(half * WIDE_LO, (half + 1) * WIDE_LO)
            value = arrived[:, 8 * half : 8 * half + 8, :].reshape(16, WIDE_LO)
            g[xx, yy, cc, 16 * h : 16 * h + 16, lanes] = value.astype(BF16)
        loop(1, NX * NY, lambda k: g_copy(h, k).start())

    def m_copy(h, core):
        here = g.at[:, :, core, group_rows(h)]
        return remote(here, here, m_send.at[h], m_recv.at[h], mate)

    def share(h):
        loop(1, NX * NY, lambda k: g_from(h, k).wait_recv())
        m_copy(h, cc).start()

    toks, slots = 256, 128

    def select(h):
        lane = lax.broadcasted_iota(jnp.int32, (toks, side), 1)
        row = lax.broadcasted_iota(jnp.int32, (toks, side), 0)
        mine = (lax.rem(lane, 32) == wide) & (lane < 96)
        square_r = lax.broadcasted_iota(jnp.int32, (toks, toks), 0)
        square_c = lax.broadcasted_iota(jnp.int32, (toks, toks), 1)
        lower = ((square_r // 8 == square_c // 8) & (square_c < square_r)).astype(F32).astype(BF16)
        m_copy(h, 1 - cc).wait_recv()
        for d in range(2):
            here = g[2 * d : 2 * d + 2, :, :, 16 * h : 16 * h + 16].reshape(toks, block + side)
            weight = jnp.sum(
                jnp.where(mine, here[:, block:].astype(F32), 0.0), axis=1, keepdims=True
            )
            weight = jnp.broadcast_to(weight, (toks, side))
            chosen = jnp.where(weight > 0.0, 1.0, 0.0)
            rank = dot(lower, chosen.astype(BF16)).astype(jnp.int32)
            place = rank * (toks // 8) + row // 8
            pick = jnp.where((lane == place) & (weight > 0.0), 1.0, 0.0).astype(BF16)
            sel[h, d] = pick
            wcol[h, d] = weight
            taken = lax.dot_general(
                pick, here[:, :block], (((0,), (0,)), ((), ())), preferred_element_type=F32
            )
            x[h, d] = taken.astype(BF16)

    zdev = ((wide, zs(1)), (wide, zs(NZ - 1)))
    pieces = [pl.ds(p * slots // 2, slots // 2) for p in range(2)]

    def ring(s, d):
        return lax.rem(z + NZ - s, NZ) if d == 0 else lax.rem(z + s, NZ)

    def product(h, d, chunk):
        at_cols = pl.ds(pl.multiple_of(chunk * cols, cols), cols)
        return dot(x[h, d], wg[:, at_cols]), dot(x[h, d], wu[:, at_cols])

    def rs_copy(h, d, s, p, src):
        return remote(
            src.at[pieces[p]],
            part.at[h, d, s, pieces[p]],
            rs_send.at[h, d, s, p],
            rs_recv.at[h, d, s, p],
            zdev[d],
        )

    def ag_copy(h, d, s, p, chunk):
        here = hid.at[chunk, h, d, pieces[p]]
        return remote(here, here, ag_send.at[h, d, s, p], ag_recv.at[h, d, s, p], zdev[d])

    def rs_first(h):
        for d in range(2):
            gate, up = product(h, d, ring(1, d))
            first[h, d, :, :cols] = gate.astype(BF16)
            first[h, d, :, cols:] = up.astype(BF16)
            for p in range(2):
                rs_copy(h, d, 0, p, first.at[h, d]).start()

    def rs_step(h, s):
        for d in range(2):
            gate, up = product(h, d, ring(s + 1, d))
            for p in range(2):
                rows = slice(p * slots // 2, (p + 1) * slots // 2)
                rs_copy(h, d, s - 1, p, first.at[h, d]).wait_recv()
                here = part.at[h, d, s - 1, pieces[p]]
                here[:, :cols] = (here[:, :cols].astype(F32) + gate[rows]).astype(BF16)
                here[:, cols:] = (here[:, cols:].astype(F32) + up[rows]).astype(BF16)
                rs_copy(h, d, s, p, part.at[h, d, s - 1]).start()

    def down(h, d, chunk):
        at_cols = pl.ds(pl.multiple_of(chunk * cols, cols), cols)
        return dot(hid[chunk, h, d], wd[at_cols, :])

    def rs_last(h):
        for d in range(2):
            gate, up = product(h, d, z)
            for p in range(2):
                rows = slice(p * slots // 2, (p + 1) * slots // 2)
                rs_copy(h, d, NZ - 2, p, first.at[h, d]).wait_recv()
                here = part.at[h, d, NZ - 2, pieces[p]]
                gates = gate[rows] + here[:, :cols].astype(F32)
                ups = up[rows] + here[:, cols:].astype(F32)
                hid[z, h, d, pieces[p], :] = (gates / (1.0 + jnp.exp(-gates)) * ups).astype(BF16)
                ag_copy(h, d, 0, p, z).start()
        for d in range(2):
            acc[h, d] = down(h, d, z)

    def ag_step(h, s):
        for d in range(2):
            for p in range(2):
                ag_copy(h, d, s - 1, p, ring(s, d)).wait_recv()
                ag_copy(h, d, s, p, ring(s, d)).start()
        for d in range(2):
            acc[h, d] = acc[h, d] + down(h, d, ring(s, d))

    def cm_copy(h, core):
        return remote(c.at[h, :, :, core], core_in.at[h], cm_send.at[h], cm_recv.at[h], mate)

    def ag_last(h):
        for d in range(2):
            chunk = ring(NZ - 1, d)
            for p in range(2):
                ag_copy(h, d, NZ - 2, p, chunk).wait_recv()
            expert_out = (acc[h, d] + down(h, d, chunk)).astype(BF16)
            mixed = dot(sel[h, d], expert_out) * wcol[h, d][:, :1]
            c[h, 2 * d : 2 * d + 2] = mixed.astype(BF16).reshape(2, NY, NC, 16, block)
        cm_copy(h, 1 - cc).start()

    def r_copy(h, k):
        px, py = chip(k)
        return remote(
            c.at[h, px, py, cc],
            land.at[h, xx, yy],
            r_send.at[h, k],
            r_recv.at[h, k],
            (at(px, py, cc), z),
        )

    def r_from(h, k):
        px, py = chip_back(k)
        return remote(
            c.at[h, px, py, cc],
            land.at[h, px, py],
            r_send.at[h, k],
            r_recv.at[h, k],
            (at(px, py, cc), z),
        )

    def spread(h):
        cm_copy(h, cc).wait_recv()
        for px in range(NX):
            both = c[h, px, :, cc].astype(F32) + core_in[h, px].astype(F32)
            c[h, px, :, cc] = both.astype(BF16)
        land[h, xx, yy] = c[h, xx, yy, cc]
        loop(1, NX * NY, lambda k: r_copy(h, k).start())

    def b_copy(h, j):
        to = 2 * h + j
        return remote(zout.at[h, j], zback.at[z], b_send.at[h, j], b_recv.at[z], (wide, to))

    def collect(h):
        loop(1, NX * NY, lambda k: r_from(h, k).wait_recv())
        total = jnp.sum(land[h].reshape(NX * NY, 16, block).astype(F32), axis=0)
        lo = total[:, :WIDE_LO].reshape(2, 8, WIDE_LO)
        hi = total[:, WIDE_LO:].reshape(2, 8, block - WIDE_LO)
        hi = jnp.concatenate([hi, jnp.zeros((2, 8, 2 * WIDE_LO - block), F32)], axis=2)
        zout[h] = jnp.concatenate([lo, hi], axis=1).astype(BF16)
        for j in range(2):
            pl.when(z != 2 * h + j)(lambda j=j: b_copy(h, j).start())

            @pl.when(z == 2 * h + j)
            def _(j=j):
                zback[z] = zout[h, j]

    for h in range(GROUPS):
        prepare(h)
    loads[0].wait()
    loads[1].wait()
    for h in range(2):
        share(h)
        select(h)
        rs_first(h)

    def rs_pair(s):
        rs_step(0, s)
        rs_step(1, s)

    loop(1, 3, rs_pair)
    share(2)
    loop(3, 4, rs_pair)
    select(2)
    loop(4, 5, rs_pair)
    share(3)
    loop(5, 6, rs_pair)
    select(3)
    loop(6, NZ - 1, rs_pair)
    loads[2].wait()
    for h in range(2):
        rs_last(h)
        rs_first(h + 2)

    def both_pairs(s):
        for h in range(2):
            ag_step(h, s)
            rs_step(h + 2, s)

    loop(1, NZ - 1, both_pairs)
    for h in range(2):
        ag_last(h)
        rs_last(h + 2)

    def ag_pair(s):
        ag_step(2, s)
        ag_step(3, s)

    loop(1, 3, ag_pair)
    spread(0)
    loop(3, 4, ag_pair)
    spread(1)
    loop(4, 5, ag_pair)
    collect(0)
    loop(5, 6, ag_pair)
    collect(1)
    loop(6, NZ - 1, ag_pair)
    ag_last(2)
    ag_last(3)
    spread(2)
    spread(3)
    collect(2)
    collect(3)

    def b_from(src):
        return remote(
            zout.at[0, 0], zback.at[src], b_send.at[0, 0], b_recv.at[src], (wide, src)
        )

    loop(1, NZ, lambda k: b_from(zs(k)).wait_recv())
    line = []
    for n in range(NZ):
        got = zback[n].astype(F32)
        line += [got[:8, :], got[8:, : block - WIDE_LO]]
    out[...] = jnp.concatenate(line, axis=1).astype(BF16)

    loop(1, NZ, lambda k: z_copy(zs(k)).wait_send())
    for h in range(GROUPS):
        loop(1, NX * NY, lambda k: g_copy(h, k).wait_send())
        m_copy(h, cc).wait_send()
        cm_copy(h, 1 - cc).wait_send()
        loop(1, NX * NY, lambda k: r_copy(h, k).wait_send())
        for j in range(2):
            pl.when(z != 2 * h + j)(lambda j=j: b_copy(h, j).wait_send())

    def drain(s):
        for h in range(GROUPS):
            for d in range(2):
                for p in range(2):
                    rs_copy(h, d, s, p, first.at[h, d]).wait_send()
                    ag_copy(h, d, s, p, ring(s, d)).wait_send()

    loop(0, NZ - 1, drain)


def on_device(tokens, routes, gates, fallback, w_gate, w_up, w_down):
    experts = lax.axis_size("wide")
    narrow = lax.axis_size("narrow")
    tok_rows, width = tokens.shape
    block = width // narrow
    ff = w_gate.shape[2]
    capacity = min(tok_rows // 2, tok_rows * routes.shape[1] // experts)
    rows = experts * narrow * 2 * capacity
    cols = ff // narrow
    slots = rows // (2 * GROUPS)

    expert_ids = jnp.arange(experts, dtype=jnp.int32)
    matched = routes[:, :, None] == expert_ids[None, None, :]
    hits = jnp.sum(matched.astype(jnp.int32), axis=1)
    weight_of = jnp.sum(jnp.where(matched, gates[:, :, None], 0.0), axis=1)
    ranks = jnp.cumsum(hits, axis=0) - hits
    primary = jnp.where(ranks < capacity, weight_of, 0.0)
    overflow = jnp.where(ranks < capacity, 0.0, weight_of)
    redirect = fallback[:, None] == expert_ids[None, :]
    weights = primary + jnp.sum(jnp.where(redirect[None], overflow[:, :, None], 0.0), axis=1)
    high = lax.reduce_precision(weights, 8, 7)
    middle = lax.reduce_precision(weights - high, 8, 7)
    low = weights - high - middle
    side = jnp.concatenate([high, middle, low, jnp.zeros_like(low)], axis=1).astype(BF16)
    pieces = tokens.reshape(tok_rows, narrow, block).transpose(1, 0, 2)
    side = jnp.broadcast_to(side[None], (narrow, tok_rows, SIDE))
    tok = jnp.concatenate(
        [pieces[:, :, :WIDE_LO], jnp.concatenate([pieces[:, :, WIDE_LO:], side], axis=2)], axis=1
    )

    vmem = pl.BlockSpec(memory_space=pltpu.VMEM)
    hbm = pl.BlockSpec(memory_space=pl.ANY)
    line = block + SIDE
    dma = pltpu.SemaphoreType.DMA
    return pl.pallas_call(
        kernel,
        out_shape=jax.ShapeDtypeStruct((tok_rows, width), BF16),
        in_specs=[vmem, hbm, hbm, hbm],
        out_specs=vmem,
        scratch_shapes=[
            pltpu.VMEM((NZ, 16, WIDE_LO), BF16),
            pltpu.VMEM((NX, NY, NC, 64, line), BF16),
            pltpu.VMEM((GROUPS, 2, slots, block), BF16),
            pltpu.VMEM((GROUPS, 2, 256, slots), BF16),
            pltpu.VMEM((GROUPS, 2, 256, SIDE), F32),
            pltpu.VMEM((block, ff), BF16),
            pltpu.VMEM((block, ff), BF16),
            pltpu.VMEM((ff, block), BF16),
            pltpu.VMEM((GROUPS, 2, slots, 2 * cols), BF16),
            pltpu.VMEM((GROUPS, 2, NZ - 1, slots, 2 * cols), BF16),
            pltpu.VMEM((NZ, GROUPS, 2, slots, cols), BF16),
            pltpu.VMEM((GROUPS, 2, slots, block), F32),
            pltpu.VMEM((GROUPS, NX, NY, NC, 16, block), BF16),
            pltpu.VMEM((GROUPS, NX, NY, 16, block), BF16),
            pltpu.VMEM((GROUPS, NX, NY, 16, block), BF16),
            pltpu.VMEM((GROUPS, 2, 16, WIDE_LO), BF16),
            pltpu.VMEM((NZ, 16, WIDE_LO), BF16),
            dma((3,)),
            dma((NZ,)),
            dma((NZ,)),
            dma((GROUPS, NX * NY)),
            dma((GROUPS, NX * NY)),
            dma((GROUPS,)),
            dma((GROUPS,)),
            dma((GROUPS, 2, NZ - 1, 2)),
            dma((GROUPS, 2, NZ - 1, 2)),
            dma((GROUPS, 2, NZ - 1, 2)),
            dma((GROUPS, 2, NZ - 1, 2)),
            dma((GROUPS,)),
            dma((GROUPS,)),
            dma((GROUPS, NX * NY)),
            dma((GROUPS, NX * NY)),
            dma((GROUPS, 2)),
            dma((NZ,)),
        ],
        compiler_params=pltpu.CompilerParams(
            collective_id=0, has_side_effects=True, vmem_limit_bytes=58 * 1024 * 1024
        ),
        cost_estimate=pl.CostEstimate(
            flops=6 * rows * block * ff, bytes_accessed=6 * block * ff, transcendentals=rows * cols
        ),
        name="experts",
    )(tok, w_gate[0], w_up[0], w_down[0])


def solution(mesh):
    placed = (
        P(("wide", "narrow"), None),
        P(("wide", "narrow"), None),
        P(("wide", "narrow"), None),
        P(),
        P("wide", "narrow", None),
        P("wide", "narrow", None),
        P("wide", None, "narrow"),
    )
    return jax.shard_map(
        on_device,
        mesh=mesh,
        in_specs=placed,
        out_specs=P(("wide", "narrow"), None),
        check_vma=False,
    )
```

```python
import functools

import jax
import jax.numpy as jnp
from jax import lax
from jax.experimental import pallas as pl
from jax.experimental.pallas import tpu as pltpu
from jax.sharding import PartitionSpec as P

F32 = jnp.float32
BF16 = jnp.bfloat16
NX, NY, NC, NZ = 4, 4, 2, 8
SIDE = 128
WIDE_LO = 512
GROUPS = 4
PIECES = 4
SUBS = 4
BOUNDS = (0, 112, 208, 304, 400)
ROWS = BOUNDS[-1]


def dot(a, b):
    return jnp.dot(a, b, preferred_element_type=F32)


def kernel(
    tok,
    wg_hbm,
    wu_hbm,
    wd_hbm,
    out,
    load,
    zin,
    g,
    x,
    sel,
    wrow,
    own0,
    w1,
    w2,
    first,
    part,
    hid,
    acc,
    c,
    core_in,
    land,
    zout,
    zback,
    wl,
    ws,
    wr,
    z_send,
    z_recv,
    g_send,
    g_recv,
    m_send,
    m_recv,
    rs_send,
    rs_recv,
    ag_send,
    ag_recv,
    cm_send,
    cm_recv,
    r_send,
    r_recv,
    b_send,
    b_recv,
):
    wide, z = lax.axis_index("wide"), lax.axis_index("narrow")
    cc = lax.rem(wide, NC)
    yy = lax.rem(wide // NC, NY)
    xx = wide // (NC * NY)
    block = x.shape[2] // 2
    rows = x.shape[1]
    cols = w1.shape[2] // 2
    part_ff = NZ * cols
    side = g.shape[4] - block

    def at(px, py, pc):
        return (px * NY + py) * NC + pc

    def zs(k):
        return lax.rem(z + k, NZ)

    def chip(k):
        return lax.rem(xx + k // NY, NX), lax.rem(yy + lax.rem(k, NY), NY)

    def chip_back(k):
        return lax.rem(xx + NX - k // NY, NX), lax.rem(yy + NY - lax.rem(k, NY), NY)

    mate = (at(xx, yy, 1 - cc), z)

    def remote(src, dst, send, recv, device):
        return pltpu.make_async_remote_copy(
            src_ref=src,
            dst_ref=dst,
            send_sem=send,
            recv_sem=recv,
            device_id=device,
            device_id_type=pl.DeviceIdType.MESH,
        )

    def loop(lo, hi, body):
        def step(i, carry):
            body(i)
            return carry

        lax.fori_loop(lo, hi, step, 0)

    def w_refs(i, k, half, owner):
        lanes = pl.ds(pl.multiple_of(half * part_ff + k * cols, cols), cols)
        deep = pl.ds(pl.multiple_of(owner * block, block), block)
        if i < 2:
            src = (wg_hbm, wu_hbm)[i].at[:, lanes]
            return src, w1.at[k, deep, pl.ds(i * cols, cols)]
        return wd_hbm.at[lanes, :], w2.at[k, pl.ds(pl.multiple_of(owner * cols, cols), cols)]

    def w_load(i, k):
        src, dst = w_refs(i, k, cc, cc)
        return pltpu.make_async_copy(src, dst, wl.at[i, k])

    def w_give(i, k):
        src, dst = w_refs(i, k, 1 - cc, cc)
        return remote(src, dst, ws.at[i, k], wr.at[i, k], mate)

    def w_get(i, k):
        src, dst = w_refs(i, k, cc, 1 - cc)
        return remote(src, dst, ws.at[i, k], wr.at[i, k], mate)

    for i in range(3):
        loop(0, NZ, lambda k: w_load(i, k).start())

    barrier = pltpu.get_barrier_semaphore()

    def greet(device):
        pl.semaphore_signal(barrier, inc=1, device_id=device, device_id_type=pl.DeviceIdType.MESH)

    for k in range(1, NZ):
        greet((wide, zs(k)))
    greet(mate)
    loop(1, NX * NY, lambda k: greet((at(*chip(k), cc), z)))
    pl.semaphore_wait(barrier, NZ - 1 + 1 + NX * NY - 1)

    def z_copy(to):
        return remote(tok.at[to], zin.at[z], z_send.at[to], z_recv.at[z], (wide, to))

    def z_from(src):
        return remote(tok.at[src], zin.at[src], z_send.at[src], z_recv.at[src], (wide, src))

    loop(1, NZ, lambda k: z_copy(zs(k)).start())
    zin[z] = tok[z]
    for i in range(3):
        loop(0, NZ, lambda k: w_give(i, k).start())

    def group_rows(h):
        return pl.ds(16 * h, 16)

    def g_copy(h, k):
        px, py = chip(k)
        here = g.at[xx, yy, cc, group_rows(h)]
        return remote(here, here, g_send.at[h, k], g_recv.at[h, k], (at(px, py, cc), z))

    def g_from(h, k):
        px, py = chip_back(k)
        there = g.at[px, py, cc, group_rows(h)]
        return remote(there, there, g_send.at[h, k], g_recv.at[h, k], (at(px, py, cc), z))

    def prepare(h):
        for src in (2 * h, 2 * h + 1):
            pl.when(z != src)(lambda src=src: z_from(src).wait_recv())
        arrived = zin[2 * h : 2 * h + 2].astype(F32)
        for half in range(2):
            lanes = slice(half * WIDE_LO, (half + 1) * WIDE_LO)
            value = arrived[:, 8 * half : 8 * half + 8, :].reshape(16, WIDE_LO)
            g[xx, yy, cc, 16 * h : 16 * h + 16, lanes] = value.astype(BF16)

    def spread_tokens(h):
        loop(1, NX * NY, lambda k: g_copy(h, k).start())

    def m_copy(h, core):
        here = g.at[:, :, core, group_rows(h)]
        return remote(here, here, m_send.at[h], m_recv.at[h], mate)

    def share(h):
        loop(1, NX * NY, lambda k: g_from(h, k).wait_recv())
        m_copy(h, cc).start()

    toks = 512
    expert0 = wide - cc

    def select(h):
        m_copy(h, 1 - cc).wait_recv()
        here = g[:, :, :, 16 * h : 16 * h + 16].reshape(toks, block + side)
        weights = here[:, block:].astype(F32)
        lane = lax.broadcasted_iota(jnp.int32, (toks, side), 1)

        def weight_of(expert):
            mine = (lax.rem(lane, 32) == expert) & (lane < 96)
            return jnp.sum(jnp.where(mine, weights, 0.0), axis=1, keepdims=True)

        chosen = [jnp.where(weight_of(expert0 + j) > 0.0, 1.0, 0.0) for j in range(2)]
        both = jnp.where(lane < side // 2, chosen[0], chosen[1]).astype(BF16)
        square_r = lax.broadcasted_iota(jnp.int32, (toks, toks), 0)
        square_c = lax.broadcasted_iota(jnp.int32, (toks, toks), 1)
        lower = jnp.where(square_c < square_r, 1.0, 0.0).astype(BF16)
        before = dot(lower, both)
        total0 = jnp.sum(chosen[0], axis=0, keepdims=True)
        place0 = jnp.where(chosen[0] > 0.0, before[:, :1], -1.0).astype(jnp.int32)
        place1 = jnp.where(chosen[1] > 0.0, before[:, side // 2 : side // 2 + 1] + total0, -1.0)
        place1 = place1.astype(jnp.int32)
        slot = lax.broadcasted_iota(jnp.int32, (toks, rows), 1)
        pick = jnp.where((slot == place0) | (slot == place1), 1.0, 0.0).astype(BF16)
        sel[h] = pick
        taken = lax.dot_general(pick, here, (((0,), (0,)), ((), ())), preferred_element_type=F32)
        row = lax.broadcasted_iota(jnp.int32, (rows, side), 0)
        lane = lax.broadcasted_iota(jnp.int32, (rows, side), 1)
        is0 = row < total0.astype(jnp.int32)
        own0[h] = jnp.where(is0, 1.0, 0.0).astype(BF16)
        mine = (lax.rem(lane, 32) == jnp.where(is0, expert0, expert0 + 1)) & (lane < 96)
        weight = jnp.sum(jnp.where(mine, taken[:, block:], 0.0), axis=1, keepdims=True)
        wrow[h] = jnp.broadcast_to(weight, (rows, side))
        first0 = is0[:, :1]
        x[h, :, :block] = jnp.where(first0, taken[:, :block], 0.0).astype(BF16)
        x[h, :, block:] = jnp.where(first0, 0.0, taken[:, :block]).astype(BF16)

        pair_r = lax.broadcasted_iota(jnp.int32, (side, side), 0)
        pair_c = lax.broadcasted_iota(jnp.int32, (side, side), 1)
        pair = jnp.where((pair_r < 32) & (pair_r // 2 == pair_c // 2), 1.0, 0.0).astype(BF16)
        any_chip = dot(jnp.where(weights > 0.0, 1.0, 0.0).astype(BF16), pair)
        count = jnp.broadcast_to(jnp.sum(any_chip, axis=0, keepdims=True), (8, side))
        load[...] = count if h == 0 else jnp.maximum(load[...], count)

    far = NZ // 2
    zdev = ((wide, zs(1)), (wide, zs(NZ - 1)))

    def rows_of(p):
        return pl.ds(BOUNDS[p], BOUNDS[p + 1] - BOUNDS[p])

    def halfway(d, p):
        return p // (PIECES // 2) == d

    def ring(s, d):
        return lax.rem(z + NZ - s, NZ) if d == 0 else lax.rem(z + s, NZ)

    def product(h, here, chunk):
        return dot(x[h, here, :], w1[chunk])

    def rs_copy(h, d, s, p):
        src = first.at[h, d, pl.ds(BOUNDS[p] - BOUNDS[d * (PIECES // 2)], BOUNDS[p + 1] - BOUNDS[p])] if s == 0 else part.at[h, d, s - 1, rows_of(p)]
        return remote(
            src,
            part.at[h, d, s, rows_of(p)],
            rs_send.at[h, d, s, p],
            rs_recv.at[h, d, s, p],
            zdev[d],
        )

    def rs_wait(h, d, s, p):
        here = part.at[h, d, s, rows_of(p)]
        remote(here, here, rs_send.at[h, d, s, p], rs_recv.at[h, d, s, p], zdev[d]).wait_recv()

    def rs_sent(h, d, s, p):
        here = part.at[h, d, s, rows_of(p)]
        remote(here, here, rs_send.at[h, d, s, p], rs_recv.at[h, d, s, p], zdev[d]).wait_send()

    def ag_copy(h, d, s, p, chunk):
        here = hid.at[chunk, h, rows_of(p)]
        return remote(here, here, ag_send.at[h, d, s, p], ag_recv.at[h, d, s, p], zdev[d])

    def rs_first(h):
        for d in range(2):
            lo, hi = BOUNDS[d * (PIECES // 2)], BOUNDS[(d + 1) * (PIECES // 2)]
            value = product(h, slice(lo, hi), ring(far, d))
            first[h, d, : hi - lo, :] = value.astype(BF16)
            for p in range(PIECES):
                if halfway(d, p):
                    rs_copy(h, d, 0, p).start()

    def rs_step(h, s, opening=False):
        for d in range(2):
            value = product(h, slice(None), ring(NZ - far + s, d))
            for p in range(PIECES):
                own = value[BOUNDS[p] : BOUNDS[p + 1]]
                here = part.at[h, d, s - 1, rows_of(p)]
                if opening and not halfway(d, p):
                    here[...] = own.astype(BF16)
                else:
                    rs_wait(h, d, s - 1, p)
                    here[...] = (here[...].astype(F32) + own).astype(BF16)
                rs_copy(h, d, s, p).start()

    def down(h, chunk):
        hidden = hid[chunk, h].astype(F32)
        mask = own0[h].astype(F32)
        apart = jnp.concatenate([hidden * mask, hidden * (1.0 - mask)], axis=1)
        return dot(apart.astype(BF16), w2[chunk])

    def rs_last(h):
        value = product(h, slice(None), z)
        for p in range(PIECES):
            total = value[BOUNDS[p] : BOUNDS[p + 1]]
            for d in range(2):
                rs_wait(h, d, far - 1, p)
                total = total + part[h, d, far - 1, rows_of(p), :].astype(F32)
            gate, up = total[:, :cols], total[:, cols:]
            hid[z, h, rows_of(p), :] = (gate / (1.0 + jnp.exp(-gate)) * up).astype(BF16)
            for d in range(2):
                ag_copy(h, d, 0, p, z).start()

    def ag_own(h):
        acc[h % 2] = down(h, z)

    def ag_pass(h, s, closing=False):
        for p in range(PIECES):
            for d in range(2):
                ag_copy(h, d, s - 1, p, ring(s, d)).wait_recv()
                if not closing or halfway(d, p):
                    ag_copy(h, d, s, p, ring(s, d)).start()

    def ag_down(h, s):
        acc[h % 2] = acc[h % 2] + down(h, ring(s, 0)) + down(h, ring(s, 1))

    def cm_copy(h, core):
        return remote(c.at[h, :, :, core], core_in.at[h], cm_send.at[h], cm_recv.at[h], mate)

    def ag_last(h):
        for p in range(PIECES):
            for d in range(2):
                if halfway(d, p):
                    ag_copy(h, d, far - 1, p, ring(far, d)).wait_recv()
        weighted = (acc[h % 2] + down(h, ring(far, 0))) * wrow[h][:, :1]
        mixed = dot(sel[h], weighted.astype(BF16))
        c[h] = mixed.astype(BF16).reshape(NX, NY, NC, 16, block)
        cm_copy(h, 1 - cc).start()

    def r_copy(h, k):
        px, py = chip(k)
        return remote(
            c.at[h, px, py, cc],
            land.at[h, xx, yy],
            r_send.at[h, k],
            r_recv.at[h, k],
            (at(px, py, cc), z),
        )

    def r_from(h, k):
        px, py = chip_back(k)
        return remote(
            c.at[h, px, py, cc],
            land.at[h, px, py],
            r_send.at[h, k],
            r_recv.at[h, k],
            (at(px, py, cc), z),
        )

    def spread(h):
        cm_copy(h, cc).wait_recv()
        for px in range(NX):
            both = c[h, px, :, cc].astype(F32) + core_in[h, px].astype(F32)
            c[h, px, :, cc] = both.astype(BF16)
        land[h, xx, yy] = c[h, xx, yy, cc]
        loop(1, NX * NY, lambda k: r_copy(h, k).start())

    def b_copy(h, j):
        to = 2 * h + j
        return remote(zout.at[h, j], zback.at[z], b_send.at[h, j], b_recv.at[z], (wide, to))

    def collect(h):
        loop(1, NX * NY, lambda k: r_from(h, k).wait_recv())
        total = jnp.sum(land[h].reshape(NX * NY, 16, block).astype(F32), axis=0)
        lo = total[:, :WIDE_LO].reshape(2, 8, WIDE_LO)
        hi = total[:, WIDE_LO:].reshape(2, 8, block - WIDE_LO)
        hi = jnp.concatenate([hi, jnp.zeros((2, 8, 2 * WIDE_LO - block), F32)], axis=2)
        zout[h] = jnp.concatenate([lo, hi], axis=1).astype(BF16)
        for j in range(2):
            pl.when(z != 2 * h + j)(lambda j=j: b_copy(h, j).start())

            @pl.when(z == 2 * h + j)
            def _(j=j):
                zback[z] = zout[h, j]

    prepare(0)
    spread_tokens(0)
    for h in range(1, GROUPS):
        prepare(h)
    share(0)
    spread_tokens(1)
    for i in range(2):
        loop(0, NZ, lambda k: w_load(i, k).wait())
        loop(0, NZ, lambda k: w_get(i, k).wait_recv())
    select(0)
    rs_first(0)
    share(1)
    spread_tokens(2)
    rs_step(0, 1, opening=True)
    select(1)
    rs_first(1)
    rs_step(1, 1, opening=True)
    share(2)
    spread_tokens(3)
    for h in range(2):
        rs_step(h, 2)
    select(2)
    share(3)
    for h in range(2):
        rs_step(h, 3)
    select(3)
    loop(0, NZ, lambda k: w_load(2, k).wait())
    loop(0, NZ, lambda k: w_get(2, k).wait_recv())
    for h in range(2):
        rs_first(h + 2)
        rs_last(h)
    for h in range(2):
        ag_own(h)
    for s in range(1, far):
        for h in range(2):
            ag_pass(h, s, closing=s == far - 1)
            rs_step(h + 2, s, opening=s == 1)
            ag_down(h, s)
    for h in range(2):
        rs_last(h + 2)
        ag_last(h)
    for h in range(2, 4):
        ag_own(h)
    for s in range(1, far):
        for h in range(2, 4):
            ag_pass(h, s, closing=s == far - 1)
        for h in range(2, 4):
            ag_down(h, s)
        if s < 3:
            spread(s - 1)
        else:
            collect(0)
            collect(1)
    ag_last(2)
    ag_last(3)
    spread(2)
    spread(3)
    collect(2)
    collect(3)

    def b_from(src):
        return remote(
            zout.at[0, 0], zback.at[src], b_send.at[0, 0], b_recv.at[src], (wide, src)
        )

    loop(1, NZ, lambda k: b_from(zs(k)).wait_recv())
    line = []
    for n in range(NZ):
        got = zback[n].astype(F32)
        line += [got[:8, :], got[8:, : block - WIDE_LO]]
    out[...] = jnp.concatenate(line, axis=1).astype(BF16)

    loop(1, NZ, lambda k: z_copy(zs(k)).wait_send())
    for i in range(3):
        loop(0, NZ, lambda k: w_give(i, k).wait_send())
    for h in range(GROUPS):
        loop(1, NX * NY, lambda k: g_copy(h, k).wait_send())
        m_copy(h, cc).wait_send()
        cm_copy(h, 1 - cc).wait_send()
        loop(1, NX * NY, lambda k: r_copy(h, k).wait_send())
        for j in range(2):
            pl.when(z != 2 * h + j)(lambda j=j: b_copy(h, j).wait_send())

    for h in range(GROUPS):
        for d in range(2):
            for s in range(far):
                for p in range(PIECES):
                    if s > 0 or halfway(d, p):
                        rs_sent(h, d, s, p)
                    if s < far - 1 or halfway(d, p):
                        ag_copy(h, d, s, p, z).wait_send()


class Copies:
    def __init__(self, send, recv):
        self.send, self.recv = send, recv
        self.used = 0
        self.started = []

    def slot(self):
        self.used += 1
        return self.used - 1

    def make(self, slot, src, dst, device):
        return pltpu.make_async_remote_copy(
            src_ref=src,
            dst_ref=dst,
            send_sem=self.send.at[slot],
            recv_sem=self.recv.at[slot],
            device_id=device,
            device_id_type=pl.DeviceIdType.MESH,
        )

    def go(self, slot, src, dst, device):
        copy = self.make(slot, src, dst, device)
        copy.start()
        self.started.append(copy)


def every_slot_kernel(
    tok,
    wg_hbm,
    wu_hbm,
    wd_hbm,
    out,
    zin,
    g,
    x,
    sel,
    wcol,
    wg,
    wu,
    wd,
    first,
    part,
    hid,
    acc,
    c,
    core_in,
    ra1,
    ra2,
    rb1,
    rb2,
    zout,
    zback,
    load_sem,
    send,
    recv,
    rs_send,
    rs_recv,
    ag_send,
    ag_recv,
):
    wide, z = lax.axis_index("wide"), lax.axis_index("narrow")
    cc = lax.rem(wide, NC)
    yy = lax.rem(wide // NC, NY)
    xx = wide // (NC * NY)
    block = x.shape[1]
    rows = x.shape[0]
    half = rows // 2
    sub = half // SUBS
    cols = wg.shape[1] // NZ

    def at(px, py, pc):
        return (px * NY + py) * NC + pc

    def xs(k):
        return lax.rem(xx + k, NX)

    def ys(k):
        return lax.rem(yy + k, NY)

    def zs(k):
        return lax.rem(z + k, NZ)

    xdev = {1: (at(xs(1), yy, cc), z), -1: (at(xs(3), yy, cc), z)}
    ydev = {1: (at(xx, ys(1), cc), z), -1: (at(xx, ys(3), cc), z)}
    mate = (at(xx, yy, 1 - cc), z)

    loads = [
        pltpu.make_async_copy(a, b, load_sem.at[i])
        for i, (a, b) in enumerate(((wg_hbm, wg), (wu_hbm, wu), (wd_hbm, wd)))
    ]
    for load in loads:
        load.start()

    barrier = pltpu.get_barrier_semaphore()
    peers = [xdev[1], xdev[-1], ydev[1], ydev[-1], mate] + [(wide, zs(k)) for k in range(1, NZ)]
    for peer in peers:
        pl.semaphore_signal(barrier, inc=1, device_id=peer, device_id_type=pl.DeviceIdType.MESH)
    pl.semaphore_wait(barrier, len(peers))

    copies = Copies(send, recv)

    zslots = {}
    for k in range(1, NZ):
        zslots[k] = copies.slot()
        copies.go(zslots[k], tok.at[zs(k)], zin.at[z], (wide, zs(k)))
    zin[z] = tok[z]
    for k in range(1, NZ):
        src = zs(NZ - k)
        copies.make(zslots[k], tok.at[src], zin.at[src], (wide, src)).wait_recv()
    arrived = zin[...].astype(F32)
    tokens_z = arrived.shape[0] * arrived.shape[1] // 2
    g[xx, yy, cc, :, :WIDE_LO] = arrived[:, :8, :].reshape(tokens_z, WIDE_LO).astype(BF16)
    g[xx, yy, cc, :, WIDE_LO:] = arrived[:, 8:, :].reshape(tokens_z, WIDE_LO).astype(BF16)

    def lane_a(pos):
        return lambda lo, n: g.at[pos, yy, cc, pl.ds(lo, n)]

    def lane_b(pos):
        return lambda lo, n: g.at[xx, pos, cc, pl.ds(32 + lo, n)]

    def plane_a(pos):
        return lambda lo, n: g.at[:, pos, cc, pl.ds(lo, n)]

    def plane_b(pos):
        return lambda lo, n: g.at[pos, :, cc, pl.ds(32 + lo, n)]

    def gather_start(region, step, dev):
        right, left = copies.slot(), copies.slot()
        own = region(step(0))(0, 32)
        copies.go(right, own, own, dev[1])
        copies.go(left, own, own, dev[-1])
        return right, left

    def gather_forward(region, step, dev, slots):
        right, left = copies.slot(), copies.slot()
        before, after = region(step(3)), region(step(1))
        copies.make(slots[0], before(0, 32), before(0, 32), dev[-1]).wait_recv()
        copies.go(right, before(0, 16), before(0, 16), dev[1])
        copies.make(slots[1], after(0, 32), after(0, 32), dev[1]).wait_recv()
        copies.go(left, after(16, 16), after(16, 16), dev[-1])
        return right, left

    def gather_end(region, step, dev, slots):
        far = region(step(2))
        copies.make(slots[0], far(0, 16), far(0, 16), dev[-1]).wait_recv()
        copies.make(slots[1], far(16, 16), far(16, 16), dev[1]).wait_recv()

    core_waits = []

    def to_mate(region, step, k):
        slot = copies.slot()
        copies.go(slot, region(step(k))(0, 32), region(step(k))(0, 32), mate)
        core_waits.append((slot, region, step, k))

    a1 = gather_start(lane_a, xs, xdev)
    b1 = gather_start(lane_b, ys, ydev)
    a2 = gather_forward(lane_a, xs, xdev, a1)
    b2 = gather_forward(lane_b, ys, ydev, b1)
    gather_end(lane_a, xs, xdev, a2)
    a3 = gather_start(plane_a, ys, ydev)
    gather_end(lane_b, ys, ydev, b2)
    b3 = gather_start(plane_b, xs, xdev)
    to_mate(plane_a, ys, 0)
    to_mate(plane_b, xs, 0)
    a4 = gather_forward(plane_a, ys, ydev, a3)
    b4 = gather_forward(plane_b, xs, xdev, b3)
    for k in (1, 3):
        to_mate(plane_a, ys, k)
        to_mate(plane_b, xs, k)
    gather_end(plane_a, ys, ydev, a4)
    to_mate(plane_a, ys, 2)
    gather_end(plane_b, xs, xdev, b4)
    to_mate(plane_b, xs, 2)
    other = {
        plane_a: lambda pos: g.at[:, pos, 1 - cc, pl.ds(0, 32)],
        plane_b: lambda pos: g.at[pos, :, 1 - cc, pl.ds(32, 32)],
    }
    for slot, region, step, k in core_waits:
        there = other[region](step(k))
        copies.make(slot, there, there, mate).wait_recv()

    batches = 8
    toks = NX * NY * NC * 64 // batches
    slots = rows // batches
    devs = slots // 4
    lane = lax.broadcasted_iota(jnp.int32, (toks, SIDE), 1)
    row = lax.broadcasted_iota(jnp.int32, (toks, SIDE), 0)
    mine = (lax.rem(lane, 32) == wide) & (lane < 96)
    square_r = lax.broadcasted_iota(jnp.int32, (toks, toks), 0)
    square_c = lax.broadcasted_iota(jnp.int32, (toks, toks), 1)
    lower = ((square_r // 8 == square_c // 8) & (square_c < square_r)).astype(F32).astype(BF16)
    for b in range(batches):
        here = g[b // 2, 2 * (b % 2) : 2 * (b % 2) + 2].reshape(toks, block + SIDE)
        weight = jnp.sum(
            jnp.where(mine, here[:, block:].astype(F32), 0.0), axis=1, keepdims=True
        )
        weight = jnp.broadcast_to(weight, (toks, SIDE))
        chosen = jnp.where(weight > 0.0, 1.0, 0.0)
        rank = dot(lower, chosen.astype(BF16)).astype(jnp.int32)
        place = rank * devs + row // 8
        pick = jnp.where((lane == place) & (weight > 0.0), 1.0, 0.0).astype(BF16)
        sel[b] = pick
        wcol[b] = weight
        taken = lax.dot_general(
            pick, here[:, :block], (((0,), (0,)), ((), ())), preferred_element_type=F32
        )
        x[b * slots : (b + 1) * slots, :] = taken.astype(BF16)

    loads[0].wait()
    loads[1].wait()
    zdev = ((wide, zs(1)), (wide, zs(NZ - 1)))

    def ring(s, d):
        return lax.rem(z + NZ - s, NZ) if d == 0 else lax.rem(z + s, NZ)

    def product(d, q, chunk):
        rows_here = x[pl.ds(pl.multiple_of(d * half + q * sub, sub), sub), :]
        at_cols = pl.ds(pl.multiple_of(chunk * cols, cols), cols)
        return dot(rows_here, wg[:, at_cols]), dot(rows_here, wu[:, at_cols])

    def rs_copy(d, s, q, src):
        return pltpu.make_async_remote_copy(
            src_ref=src,
            dst_ref=part.at[d, s, q],
            send_sem=rs_send.at[d, s, q],
            recv_sem=rs_recv.at[d, s, q],
            device_id=zdev[d],
            device_id_type=pl.DeviceIdType.MESH,
        )

    def ag_copy(d, s, q, chunk):
        here = hid.at[chunk, pl.ds(pl.multiple_of(d * half + q * sub, sub), sub)]
        return pltpu.make_async_remote_copy(
            src_ref=here,
            dst_ref=here,
            send_sem=ag_send.at[d, s, q],
            recv_sem=ag_recv.at[d, s, q],
            device_id=zdev[d],
            device_id_type=pl.DeviceIdType.MESH,
        )

    def each_sub(body):
        def step(q, carry):
            for d in range(2):
                body(d, q)
            return carry

        lax.fori_loop(0, SUBS, step, 0)

    def rs_first(d, q):
        gate, up = product(d, q, ring(1, d))
        first[d, q, :, :cols] = gate.astype(BF16)
        first[d, q, :, cols:] = up.astype(BF16)
        rs_copy(d, 0, q, first.at[d, q]).start()

    each_sub(rs_first)

    def rs_step(s, carry):
        def body(d, q):
            gate, up = product(d, q, ring(s + 1, d))
            rs_copy(d, s - 1, q, first.at[d, q]).wait_recv()
            here = part.at[d, s - 1, q]
            here[:, :cols] = (here[:, :cols].astype(F32) + gate).astype(BF16)
            here[:, cols:] = (here[:, cols:].astype(F32) + up).astype(BF16)
            rs_copy(d, s, q, here).start()

        each_sub(body)
        return carry

    lax.fori_loop(1, NZ - 1, rs_step, 0)
    loads[2].wait()

    def down(d, q, chunk):
        at_rows = pl.ds(pl.multiple_of(d * half + q * sub, sub), sub)
        at_cols = pl.ds(pl.multiple_of(chunk * cols, cols), cols)
        return at_rows, dot(hid[chunk, at_rows, :], wd[at_cols, :])

    def rs_last(d, q):
        gate, up = product(d, q, z)
        rs_copy(d, NZ - 2, q, first.at[d, q]).wait_recv()
        here = part.at[d, NZ - 2, q]
        gate = gate + here[:, :cols].astype(F32)
        up = up + here[:, cols:].astype(F32)
        hidden = gate / (1.0 + jnp.exp(-gate)) * up
        at_rows = pl.ds(pl.multiple_of(d * half + q * sub, sub), sub)
        hid[z, at_rows, :] = hidden.astype(BF16)
        ag_copy(d, 0, q, z).start()
        at_rows, value = down(d, q, z)
        acc[at_rows, :] = value

    each_sub(rs_last)

    def ag_step(s, carry):
        def body(d, q):
            chunk = ring(s, d)
            ag_copy(d, s - 1, q, chunk).wait_recv()
            ag_copy(d, s, q, chunk).start()
            at_rows, value = down(d, q, chunk)
            acc[at_rows, :] = acc[at_rows, :] + value

        each_sub(body)
        return carry

    lax.fori_loop(1, NZ - 1, ag_step, 0)

    core_slots = [copies.slot() for _ in range(NX)]
    for b in range(batches):
        d, q = b // SUBS, b % SUBS
        chunk = ring(NZ - 1, d)
        ag_copy(d, NZ - 2, q, chunk).wait_recv()
        at_rows, value = down(d, q, chunk)
        expert_out = (acc[at_rows, :] + value).astype(BF16)
        mixed = dot(sel[b], expert_out) * wcol[b][:, :1]
        c[b // 2, 2 * (b % 2) : 2 * (b % 2) + 2] = mixed.astype(BF16).reshape(2, NC, 64, block)
        if b % 2 == 1:
            copies.go(core_slots[b // 2], c.at[b // 2, :, 1 - cc], core_in.at[b // 2], mate)
    for px in range(NX):
        copies.make(core_slots[px], c.at[px, :, cc], core_in.at[px], mate).wait_recv()
        c[px, :, cc] = (c[px, :, cc].astype(F32) + core_in[px].astype(F32)).astype(BF16)

    def c_plane_a(pos, lo, n):
        return c.at[:, pos, cc, pl.ds(lo, n)]

    def c_plane_b(pos, lo, n):
        return c.at[pos, :, cc, pl.ds(32 + lo, n)]

    def c_lane_a(pos, lo, n):
        return c.at[pos, yy, cc, pl.ds(lo, n)]

    def c_lane_b(pos, lo, n):
        return c.at[xx, pos, cc, pl.ds(32 + lo, n)]

    def add_into(ref, other_ref):
        ref[...] = (ref[...].astype(F32) + other_ref[...].astype(F32)).astype(BF16)

    def scatter_start(region, step, dev, buf):
        right, left = copies.slot(), copies.slot()
        copies.go(right, region(step(2), 0, 16), buf.at[0], dev[1])
        copies.go(left, region(step(2), 16, 16), buf.at[1], dev[-1])
        return right, left

    def scatter_forward(region, step, dev, buf, buf2, slots):
        right, left = copies.slot(), copies.slot()
        copies.make(slots[0], region(step(2), 0, 16), buf.at[0], dev[-1]).wait_recv()
        add_into(region(step(1), 0, 16), buf.at[0])
        copies.go(right, region(step(1), 0, 32), buf2.at[0], dev[1])
        copies.make(slots[1], region(step(2), 16, 16), buf.at[1], dev[1]).wait_recv()
        add_into(region(step(3), 16, 16), buf.at[1])
        copies.go(left, region(step(3), 0, 32), buf2.at[1], dev[-1])
        return right, left

    def scatter_end(region, step, dev, buf2, slots):
        copies.make(slots[0], region(step(0), 0, 32), buf2.at[0], dev[-1]).wait_recv()
        copies.make(slots[1], region(step(0), 0, 32), buf2.at[1], dev[1]).wait_recv()
        here = region(step(0), 0, 32)
        return here[...].astype(F32) + buf2[0].astype(F32) + buf2[1].astype(F32)

    a1 = scatter_start(c_plane_a, ys, ydev, ra1.at[0])
    b1 = scatter_start(c_plane_b, xs, xdev, ra1.at[1])
    a2 = scatter_forward(c_plane_a, ys, ydev, ra1.at[0], ra2.at[0], a1)
    b2 = scatter_forward(c_plane_b, xs, xdev, ra1.at[1], ra2.at[1], b1)
    total = scatter_end(c_plane_a, ys, ydev, ra2.at[0], a2)
    c[:, yy, cc, :32, :] = total.astype(BF16)
    a3 = scatter_start(c_lane_a, xs, xdev, rb1.at[0])
    total = scatter_end(c_plane_b, xs, xdev, ra2.at[1], b2)
    c[xx, :, cc, 32:, :] = total.astype(BF16)
    b3 = scatter_start(c_lane_b, ys, ydev, rb1.at[1])
    a4 = scatter_forward(c_lane_a, xs, xdev, rb1.at[0], rb2.at[0], a3)
    b4 = scatter_forward(c_lane_b, ys, ydev, rb1.at[1], rb2.at[1], b3)
    sums = [
        scatter_end(c_lane_a, xs, xdev, rb2.at[0], a4),
        scatter_end(c_lane_b, ys, ydev, rb2.at[1], b4),
    ]

    for i, total in enumerate(sums):
        lo = total[:, :WIDE_LO].reshape(4, 8, WIDE_LO)
        hi = total[:, WIDE_LO:].reshape(4, 8, block - WIDE_LO)
        hi = jnp.concatenate([hi, jnp.zeros((4, 8, 2 * WIDE_LO - block), F32)], axis=2)
        zout[4 * i : 4 * i + 4] = jnp.concatenate([lo, hi], axis=1).astype(BF16)
    zslots = {}
    for k in range(1, NZ):
        zslots[k] = copies.slot()
        copies.go(zslots[k], zout.at[zs(k)], zback.at[z], (wide, zs(k)))
    zback[z] = zout[z]
    for k in range(1, NZ):
        src = zs(NZ - k)
        copies.make(zslots[k], zout.at[src], zback.at[src], (wide, src)).wait_recv()
    pieces = []
    for n in range(NZ):
        got = zback[n].astype(F32)
        pieces += [got[:8, :], got[8:, : block - WIDE_LO]]
    out[...] = jnp.concatenate(pieces, axis=1).astype(BF16)

    for copy in copies.started:
        copy.wait_send()

    def drain(s, carry):
        def body(d, q):
            rs_copy(d, s, q, first.at[d, q]).wait_send()
            ag_copy(d, s, q, ring(s, d)).wait_send()

        each_sub(body)
        return carry

    lax.fori_loop(0, NZ - 1, drain, 0)


def every_slot(tok_rows, width, capacity, tok, w_gate, w_up, w_down):
    block, ff = w_gate.shape
    rows = NX * NY * NC * NZ * 2 * capacity
    half = rows // 2
    sub = half // SUBS
    cols = ff // NZ
    vmem = pl.BlockSpec(memory_space=pltpu.VMEM)
    hbm = pl.BlockSpec(memory_space=pl.ANY)
    line = block + SIDE
    copies = 7 + 24 + 4 + 16 + 7
    return pl.pallas_call(
        every_slot_kernel,
        out_shape=jax.ShapeDtypeStruct((tok_rows, width), BF16),
        in_specs=[vmem, hbm, hbm, hbm],
        out_specs=vmem,
        scratch_shapes=[
            pltpu.VMEM((NZ, 16, WIDE_LO), BF16),
            pltpu.VMEM((NX, NY, NC, 64, line), BF16),
            pltpu.VMEM((rows, block), BF16),
            pltpu.VMEM((8, 256, SIDE), BF16),
            pltpu.VMEM((8, 256, SIDE), F32),
            pltpu.VMEM((block, ff), BF16),
            pltpu.VMEM((block, ff), BF16),
            pltpu.VMEM((ff, block), BF16),
            pltpu.VMEM((2, SUBS, sub, 2 * cols), BF16),
            pltpu.VMEM((2, NZ - 1, SUBS, sub, 2 * cols), BF16),
            pltpu.VMEM((NZ, rows, cols), BF16),
            pltpu.VMEM((rows, block), F32),
            pltpu.VMEM((NX, NY, NC, 64, block), BF16),
            pltpu.VMEM((NX, NY, 64, block), BF16),
            pltpu.VMEM((2, 2, 4, 16, block), BF16),
            pltpu.VMEM((2, 2, 4, 32, block), BF16),
            pltpu.VMEM((2, 2, 16, block), BF16),
            pltpu.VMEM((2, 2, 32, block), BF16),
            pltpu.VMEM((NZ, 16, WIDE_LO), BF16),
            pltpu.VMEM((NZ, 16, WIDE_LO), BF16),
            pltpu.SemaphoreType.DMA((3,)),
            pltpu.SemaphoreType.DMA((copies,)),
            pltpu.SemaphoreType.DMA((copies,)),
            pltpu.SemaphoreType.DMA((2, NZ - 1, SUBS)),
            pltpu.SemaphoreType.DMA((2, NZ - 1, SUBS)),
            pltpu.SemaphoreType.DMA((2, NZ - 1, SUBS)),
            pltpu.SemaphoreType.DMA((2, NZ - 1, SUBS)),
        ],
        compiler_params=pltpu.CompilerParams(
            collective_id=1, has_side_effects=True, vmem_limit_bytes=58 * 1024 * 1024
        ),
        cost_estimate=pl.CostEstimate(
            flops=6 * rows * block * ff, bytes_accessed=6 * block * ff, transcendentals=rows * cols
        ),
        name="every_slot",
    )(tok, w_gate, w_up, w_down)


def on_device(tokens, routes, gates, fallback, w_gate, w_up, w_down):
    experts = lax.axis_size("wide")
    narrow = lax.axis_size("narrow")
    tok_rows, width = tokens.shape
    block = width // narrow
    ff = w_gate.shape[2]
    capacity = min(tok_rows // 2, tok_rows * routes.shape[1] // experts)
    expert_ids = jnp.arange(experts, dtype=jnp.int32)
    matched = routes[:, :, None] == expert_ids[None, None, :]
    hits = jnp.sum(matched.astype(jnp.int32), axis=1)
    weight_of = jnp.sum(jnp.where(matched, gates[:, :, None], 0.0), axis=1)
    ranks = jnp.cumsum(hits, axis=0) - hits
    primary = jnp.where(ranks < capacity, weight_of, 0.0)
    overflow = jnp.where(ranks < capacity, 0.0, weight_of)
    redirect = fallback[:, None] == expert_ids[None, :]
    weights = primary + jnp.sum(jnp.where(redirect[None], overflow[:, :, None], 0.0), axis=1)
    high = lax.reduce_precision(weights, 8, 7)
    middle = lax.reduce_precision(weights - high, 8, 7)
    low = weights - high - middle
    side = jnp.concatenate([high, middle, low, jnp.zeros_like(low)], axis=1).astype(BF16)
    pieces = tokens.reshape(tok_rows, narrow, block).transpose(1, 0, 2)
    side = jnp.broadcast_to(side[None], (narrow, tok_rows, SIDE))
    tok = jnp.concatenate(
        [pieces[:, :, :WIDE_LO], jnp.concatenate([pieces[:, :, WIDE_LO:], side], axis=2)], axis=1
    )

    weights = (w_gate[0], w_up[0], w_down[0])
    mixed, load = packed(tok, *weights)
    return lax.cond(
        jnp.max(load) > ROWS, lambda: every_slot(tok_rows, width, capacity, tok, *weights), lambda: mixed
    )


def packed(tok, w_gate, w_up, w_down):
    block, ff = w_gate.shape
    tok_rows, width = tok.shape[1] // 2, NZ * block
    cols = ff // NC // NZ
    vmem = pl.BlockSpec(memory_space=pltpu.VMEM)
    hbm = pl.BlockSpec(memory_space=pl.ANY)
    line = block + SIDE
    dma = pltpu.SemaphoreType.DMA
    half = BOUNDS[PIECES // 2]
    return pl.pallas_call(
        kernel,
        out_shape=(
            jax.ShapeDtypeStruct((tok_rows, width), BF16),
            jax.ShapeDtypeStruct((8, SIDE), F32),
        ),
        in_specs=[vmem, hbm, hbm, hbm],
        out_specs=(vmem, vmem),
        scratch_shapes=[
            pltpu.VMEM((NZ, 16, WIDE_LO), BF16),
            pltpu.VMEM((NX, NY, NC, 64, line), BF16),
            pltpu.VMEM((GROUPS, ROWS, 2 * block), BF16),
            pltpu.VMEM((GROUPS, 512, ROWS), BF16),
            pltpu.VMEM((GROUPS, ROWS, SIDE), F32),
            pltpu.VMEM((GROUPS, ROWS, SIDE), BF16),
            pltpu.VMEM((NZ, 2 * block, 2 * cols), BF16),
            pltpu.VMEM((NZ, 2 * cols, block), BF16),
            pltpu.VMEM((GROUPS, 2, half, 2 * cols), BF16),
            pltpu.VMEM((GROUPS, 2, NZ // 2, ROWS, 2 * cols), BF16),
            pltpu.VMEM((NZ, GROUPS, ROWS, cols), BF16),
            pltpu.VMEM((2, ROWS, block), F32),
            pltpu.VMEM((GROUPS, NX, NY, NC, 16, block), BF16),
            pltpu.VMEM((GROUPS, NX, NY, 16, block), BF16),
            pltpu.VMEM((GROUPS, NX, NY, 16, block), BF16),
            pltpu.VMEM((GROUPS, 2, 16, WIDE_LO), BF16),
            pltpu.VMEM((NZ, 16, WIDE_LO), BF16),
            dma((3, NZ)),
            dma((3, NZ)),
            dma((3, NZ)),
            dma((NZ,)),
            dma((NZ,)),
            dma((GROUPS, NX * NY)),
            dma((GROUPS, NX * NY)),
            dma((GROUPS,)),
            dma((GROUPS,)),
            dma((GROUPS, 2, NZ // 2, PIECES)),
            dma((GROUPS, 2, NZ // 2, PIECES)),
            dma((GROUPS, 2, NZ // 2, PIECES)),
            dma((GROUPS, 2, NZ // 2, PIECES)),
            dma((GROUPS,)),
            dma((GROUPS,)),
            dma((GROUPS, NX * NY)),
            dma((GROUPS, NX * NY)),
            dma((GROUPS, 2)),
            dma((NZ,)),
        ],
        compiler_params=pltpu.CompilerParams(
            collective_id=0, has_side_effects=True, vmem_limit_bytes=60 * 1024 * 1024
        ),
        cost_estimate=pl.CostEstimate(
            flops=6 * GROUPS * ROWS * block * ff,
            bytes_accessed=6 * block * ff,
            transcendentals=GROUPS * ROWS * cols,
        ),
        name="packed",
    )(tok, w_gate, w_up, w_down)


def solution(mesh):
    placed = (
        P(("wide", "narrow"), None),
        P(("wide", "narrow"), None),
        P(("wide", "narrow"), None),
        P(),
        P("wide", "narrow", None),
        P("wide", "narrow", None),
        P("wide", None, "narrow"),
    )
    return jax.shard_map(
        on_device,
        mesh=mesh,
        in_specs=placed,
        out_specs=P(("wide", "narrow"), None),
        check_vma=False,
    )
```

```python
import functools

import jax
import jax.numpy as jnp
from jax import lax
from jax.experimental import pallas as pl
from jax.experimental.pallas import tpu as pltpu
from jax.sharding import PartitionSpec as P

F32 = jnp.float32
BF16 = jnp.bfloat16
NX, NY, NC, NZ = 4, 4, 2, 8
SIDE = 128
WIDE_LO = 512
GROUPS = 4
PIECES = 4
SUBS = 4
BOUNDS = (0, 112, 208, 304, 400)
ROWS = BOUNDS[-1]


def dot(a, b):
    return jnp.dot(a, b, preferred_element_type=F32)


def make_rows(capacity, tokens, routes, gates, fallback, tok):
    tok_rows, chosen_count = routes.shape
    experts = fallback.shape[1]
    lane = lax.broadcasted_iota(jnp.int32, (tok_rows, experts), 1)
    row = lax.broadcasted_iota(jnp.int32, (tok_rows, experts), 0)
    hits = jnp.zeros((tok_rows, experts), F32)
    weight_of = jnp.zeros((tok_rows, experts), F32)
    for k in range(chosen_count):
        named = routes[:, k : k + 1] == lane
        hits = hits + jnp.where(named, 1.0, 0.0)
        weight_of = weight_of + jnp.where(named, gates[:, k : k + 1], 0.0)
    ranks = jnp.zeros((tok_rows, experts), F32)
    for t in range(tok_rows - 1):
        ranks = ranks + jnp.where(row > t, hits[t : t + 1, :], 0.0)
    primary = jnp.where(ranks < capacity, weight_of, 0.0)
    to = lax.broadcasted_iota(jnp.int32, (experts, experts), 0)
    redirect = jnp.where(to == fallback[...], 1.0, 0.0).astype(BF16)

    def split(value):
        terms = []
        for _ in range(3):
            terms.append(value.astype(BF16))
            value = value - terms[-1].astype(F32)
        return terms

    weights = primary
    for term in split(weight_of - primary):
        weights = weights + lax.dot_general(
            term, redirect, (((1,), (1,)), ((), ())), preferred_element_type=F32
        )
    terms = [term.astype(F32) for term in split(weights)]
    side = jnp.concatenate(terms + [jnp.zeros_like(weights)], axis=1)
    width = tokens.shape[1]
    block = width // NZ
    for n in range(NZ):
        here = tokens[:, n * block : (n + 1) * block].astype(F32)
        tail = jnp.concatenate([here[:, WIDE_LO:], side], axis=1)
        tok[n] = jnp.concatenate([here[:, :WIDE_LO], tail], axis=0).astype(BF16)


def kernel(
    capacity,
    tokens,
    routes,
    gates,
    fallback,
    wg_hbm,
    wu_hbm,
    wd_hbm,
    out,
    tok,
    load,
    zin,
    g,
    x,
    sel,
    wrow,
    own0,
    w1,
    w2,
    first,
    part,
    hid,
    acc,
    c,
    core_in,
    land,
    zout,
    zback,
    wl,
    ws,
    wr,
    z_send,
    z_recv,
    g_send,
    g_recv,
    m_send,
    m_recv,
    rs_send,
    rs_recv,
    ag_send,
    ag_recv,
    cm_send,
    cm_recv,
    r_send,
    r_recv,
    b_send,
    b_recv,
):
    wide, z = lax.axis_index("wide"), lax.axis_index("narrow")
    cc = lax.rem(wide, NC)
    yy = lax.rem(wide // NC, NY)
    xx = wide // (NC * NY)
    block = x.shape[2] // 2
    rows = x.shape[1]
    cols = w1.shape[2] // 2
    part_ff = NZ * cols
    side = g.shape[4] - block

    def at(px, py, pc):
        return (px * NY + py) * NC + pc

    def zs(k):
        return lax.rem(z + k, NZ)

    def chip(k):
        return lax.rem(xx + k // NY, NX), lax.rem(yy + lax.rem(k, NY), NY)

    def chip_back(k):
        return lax.rem(xx + NX - k // NY, NX), lax.rem(yy + NY - lax.rem(k, NY), NY)

    mate = (at(xx, yy, 1 - cc), z)

    def remote(src, dst, send, recv, device):
        return pltpu.make_async_remote_copy(
            src_ref=src,
            dst_ref=dst,
            send_sem=send,
            recv_sem=recv,
            device_id=device,
            device_id_type=pl.DeviceIdType.MESH,
        )

    def loop(lo, hi, body):
        def step(i, carry):
            body(i)
            return carry

        lax.fori_loop(lo, hi, step, 0)

    def w_refs(i, k, half, owner):
        lanes = pl.ds(pl.multiple_of(half * part_ff + k * cols, cols), cols)
        deep = pl.ds(pl.multiple_of(owner * block, block), block)
        if i < 2:
            src = (wg_hbm, wu_hbm)[i].at[:, lanes]
            return src, w1.at[k, deep, pl.ds(i * cols, cols)]
        return wd_hbm.at[lanes, :], w2.at[k, pl.ds(pl.multiple_of(owner * cols, cols), cols)]

    def w_load(i, k):
        src, dst = w_refs(i, k, cc, cc)
        return pltpu.make_async_copy(src, dst, wl.at[i, k])

    def w_give(i, k):
        src, dst = w_refs(i, k, 1 - cc, cc)
        return remote(src, dst, ws.at[i, k], wr.at[i, k], mate)

    def w_get(i, k):
        src, dst = w_refs(i, k, cc, 1 - cc)
        return remote(src, dst, ws.at[i, k], wr.at[i, k], mate)

    for i in range(3):
        loop(0, NZ, lambda k: w_load(i, k).start())

    make_rows(capacity, tokens, routes, gates, fallback, tok)

    barrier = pltpu.get_barrier_semaphore()

    def greet(device):
        pl.semaphore_signal(barrier, inc=1, device_id=device, device_id_type=pl.DeviceIdType.MESH)

    for k in range(1, NZ):
        greet((wide, zs(k)))
    greet(mate)
    loop(1, NX * NY, lambda k: greet((at(*chip(k), cc), z)))
    pl.semaphore_wait(barrier, NZ - 1 + 1 + NX * NY - 1)

    def z_copy(to):
        return remote(tok.at[to], zin.at[z], z_send.at[to], z_recv.at[z], (wide, to))

    def z_from(src):
        return remote(tok.at[src], zin.at[src], z_send.at[src], z_recv.at[src], (wide, src))

    loop(1, NZ, lambda k: z_copy(zs(k)).start())
    zin[z] = tok[z]
    for i in range(3):
        loop(0, NZ, lambda k: w_give(i, k).start())

    def group_rows(h):
        return pl.ds(16 * h, 16)

    def g_copy(h, k):
        px, py = chip(k)
        here = g.at[xx, yy, cc, group_rows(h)]
        return remote(here, here, g_send.at[h, k], g_recv.at[h, k], (at(px, py, cc), z))

    def g_from(h, k):
        px, py = chip_back(k)
        there = g.at[px, py, cc, group_rows(h)]
        return remote(there, there, g_send.at[h, k], g_recv.at[h, k], (at(px, py, cc), z))

    def prepare(h):
        for src in (2 * h, 2 * h + 1):
            pl.when(z != src)(lambda src=src: z_from(src).wait_recv())
        arrived = zin[2 * h : 2 * h + 2].astype(F32)
        for half in range(2):
            lanes = slice(half * WIDE_LO, (half + 1) * WIDE_LO)
            value = arrived[:, 8 * half : 8 * half + 8, :].reshape(16, WIDE_LO)
            g[xx, yy, cc, 16 * h : 16 * h + 16, lanes] = value.astype(BF16)

    def spread_tokens(h):
        loop(1, NX * NY, lambda k: g_copy(h, k).start())

    def m_copy(h, core):
        here = g.at[:, :, core, group_rows(h)]
        return remote(here, here, m_send.at[h], m_recv.at[h], mate)

    def share(h):
        loop(1, NX * NY, lambda k: g_from(h, k).wait_recv())
        m_copy(h, cc).start()

    toks = 512
    expert0 = wide - cc

    loads = []

    def select(h):
        m_copy(h, 1 - cc).wait_recv()
        here = g[:, :, :, 16 * h : 16 * h + 16].reshape(toks, block + side)
        weights = here[:, block:].astype(F32)
        lane = lax.broadcasted_iota(jnp.int32, (toks, side), 1)

        def weight_of(expert):
            mine = (lax.rem(lane, 32) == expert) & (lane < 96)
            return jnp.sum(jnp.where(mine, weights, 0.0), axis=1, keepdims=True)

        chosen = [jnp.where(weight_of(expert0 + j) > 0.0, 1.0, 0.0) for j in range(2)]
        both = jnp.where(lane < side // 2, chosen[0], chosen[1]).astype(BF16)
        square_r = lax.broadcasted_iota(jnp.int32, (toks, toks), 0)
        square_c = lax.broadcasted_iota(jnp.int32, (toks, toks), 1)
        lower = jnp.where(square_c < square_r, 1.0, 0.0).astype(BF16)
        before = dot(lower, both)
        total0 = jnp.sum(chosen[0], axis=0, keepdims=True)
        place0 = jnp.where(chosen[0] > 0.0, before[:, :1], -1.0).astype(jnp.int32)
        place1 = jnp.where(chosen[1] > 0.0, before[:, side // 2 : side // 2 + 1] + total0, -1.0)
        place1 = place1.astype(jnp.int32)
        slot = lax.broadcasted_iota(jnp.int32, (toks, rows), 1)
        pick = jnp.where((slot == place0) | (slot == place1), 1.0, 0.0).astype(BF16)
        sel[h] = pick
        taken = lax.dot_general(pick, here, (((0,), (0,)), ((), ())), preferred_element_type=F32)
        row = lax.broadcasted_iota(jnp.int32, (rows, side), 0)
        lane = lax.broadcasted_iota(jnp.int32, (rows, side), 1)
        is0 = row < total0.astype(jnp.int32)
        own0[h] = jnp.where(is0, 1.0, 0.0).astype(BF16)
        mine = (lax.rem(lane, 32) == jnp.where(is0, expert0, expert0 + 1)) & (lane < 96)
        weight = jnp.sum(jnp.where(mine, taken[:, block:], 0.0), axis=1, keepdims=True)
        wrow[h] = jnp.broadcast_to(weight, (rows, side))
        first0 = is0[:, :1]
        x[h, :, :block] = jnp.where(first0, taken[:, :block], 0.0).astype(BF16)
        x[h, :, block:] = jnp.where(first0, 0.0, taken[:, :block]).astype(BF16)

        pair_r = lax.broadcasted_iota(jnp.int32, (side, side), 0)
        pair_c = lax.broadcasted_iota(jnp.int32, (side, side), 1)
        pair = jnp.where((pair_r < 32) & (pair_r // 2 == pair_c // 2), 1.0, 0.0).astype(BF16)
        any_chip = dot(jnp.where(weights > 0.0, 1.0, 0.0).astype(BF16), pair)
        count = jnp.broadcast_to(jnp.sum(any_chip, axis=0, keepdims=True), (8, side))
        loads.append(count)

    far = NZ // 2
    zdev = ((wide, zs(1)), (wide, zs(NZ - 1)))

    def rows_of(p):
        return pl.ds(BOUNDS[p], BOUNDS[p + 1] - BOUNDS[p])

    def halfway(d, p):
        return p // (PIECES // 2) == d

    def ring(s, d):
        return lax.rem(z + NZ - s, NZ) if d == 0 else lax.rem(z + s, NZ)

    def product(h, here, chunk):
        return dot(x[h, here, :], w1[chunk])

    def rs_copy(h, d, s, p):
        src = first.at[h, d, pl.ds(BOUNDS[p] - BOUNDS[d * (PIECES // 2)], BOUNDS[p + 1] - BOUNDS[p])] if s == 0 else part.at[h, d, s - 1, rows_of(p)]
        return remote(
            src,
            part.at[h, d, s, rows_of(p)],
            rs_send.at[h, d, s, p],
            rs_recv.at[h, d, s, p],
            zdev[d],
        )

    def rs_wait(h, d, s, p):
        here = part.at[h, d, s, rows_of(p)]
        remote(here, here, rs_send.at[h, d, s, p], rs_recv.at[h, d, s, p], zdev[d]).wait_recv()

    def rs_sent(h, d, s, p):
        here = part.at[h, d, s, rows_of(p)]
        remote(here, here, rs_send.at[h, d, s, p], rs_recv.at[h, d, s, p], zdev[d]).wait_send()

    def ag_copy(h, d, s, p, chunk):
        here = hid.at[chunk, h, rows_of(p)]
        return remote(here, here, ag_send.at[h, d, s, p], ag_recv.at[h, d, s, p], zdev[d])

    def rs_first(h):
        for d in range(2):
            lo, hi = BOUNDS[d * (PIECES // 2)], BOUNDS[(d + 1) * (PIECES // 2)]
            value = product(h, slice(lo, hi), ring(far, d))
            first[h, d, : hi - lo, :] = value.astype(BF16)
            for p in range(PIECES):
                if halfway(d, p):
                    rs_copy(h, d, 0, p).start()

    def rs_step(h, s, opening=False):
        for d in range(2):
            value = product(h, slice(None), ring(NZ - far + s, d))
            for p in sorted(range(PIECES), key=lambda p: opening and halfway(d, p)):
                own = value[BOUNDS[p] : BOUNDS[p + 1]]
                here = part.at[h, d, s - 1, rows_of(p)]
                if opening and not halfway(d, p):
                    here[...] = own.astype(BF16)
                else:
                    rs_wait(h, d, s - 1, p)
                    here[...] = (here[...].astype(F32) + own).astype(BF16)
                rs_copy(h, d, s, p).start()

    def down(h, chunk):
        hidden = hid[chunk, h].astype(F32)
        mask = own0[h].astype(F32)
        apart = jnp.concatenate([hidden * mask, hidden * (1.0 - mask)], axis=1)
        return dot(apart.astype(BF16), w2[chunk])

    def rs_last(h):
        value = product(h, slice(None), z)
        for p in range(PIECES):
            total = value[BOUNDS[p] : BOUNDS[p + 1]]
            for d in range(2):
                rs_wait(h, d, far - 1, p)
                total = total + part[h, d, far - 1, rows_of(p), :].astype(F32)
            gate, up = total[:, :cols], total[:, cols:]
            hid[z, h, rows_of(p), :] = (gate / (1.0 + jnp.exp(-gate)) * up).astype(BF16)
            for d in range(2):
                ag_copy(h, d, 0, p, z).start()

    def ag_own(h):
        acc[h % 2] = down(h, z)

    def ag_pass(h, s, closing=False):
        for p in range(PIECES):
            for d in range(2):
                ag_copy(h, d, s - 1, p, ring(s, d)).wait_recv()
                if not closing or halfway(d, p):
                    ag_copy(h, d, s, p, ring(s, d)).start()

    def ag_down(h, s):
        acc[h % 2] = acc[h % 2] + down(h, ring(s, 0)) + down(h, ring(s, 1))

    def cm_copy(h, core):
        return remote(c.at[h, :, :, core], core_in.at[h], cm_send.at[h], cm_recv.at[h], mate)

    def ag_last(h):
        for p in range(PIECES):
            for d in range(2):
                if halfway(d, p):
                    ag_copy(h, d, far - 1, p, ring(far, d)).wait_recv()
        weighted = (acc[h % 2] + down(h, ring(far, 0))) * wrow[h][:, :1]
        mixed = dot(sel[h], weighted.astype(BF16))
        c[h] = mixed.astype(BF16).reshape(NX, NY, NC, 16, block)
        cm_copy(h, 1 - cc).start()

    def r_copy(h, k):
        px, py = chip(k)
        return remote(
            c.at[h, px, py, cc],
            land.at[h, xx, yy],
            r_send.at[h, k],
            r_recv.at[h, k],
            (at(px, py, cc), z),
        )

    def r_from(h, k):
        px, py = chip_back(k)
        return remote(
            c.at[h, px, py, cc],
            land.at[h, px, py],
            r_send.at[h, k],
            r_recv.at[h, k],
            (at(px, py, cc), z),
        )

    def spread(h):
        cm_copy(h, cc).wait_recv()
        for px in range(NX):
            both = c[h, px, :, cc].astype(F32) + core_in[h, px].astype(F32)
            c[h, px, :, cc] = both.astype(BF16)
        land[h, xx, yy] = c[h, xx, yy, cc]
        loop(1, NX * NY, lambda k: r_copy(h, k).start())

    def b_copy(h, j):
        to = 2 * h + j
        return remote(zout.at[h, j], zback.at[z], b_send.at[h, j], b_recv.at[z], (wide, to))

    def collect(h):
        loop(1, NX * NY, lambda k: r_from(h, k).wait_recv())
        total = jnp.sum(land[h].reshape(NX * NY, 16, block).astype(F32), axis=0)
        lo = total[:, :WIDE_LO].reshape(2, 8, WIDE_LO)
        hi = total[:, WIDE_LO:].reshape(2, 8, block - WIDE_LO)
        hi = jnp.concatenate([hi, jnp.zeros((2, 8, 2 * WIDE_LO - block), F32)], axis=2)
        zout[h] = jnp.concatenate([lo, hi], axis=1).astype(BF16)
        for j in range(2):
            pl.when(z != 2 * h + j)(lambda j=j: b_copy(h, j).start())

            @pl.when(z == 2 * h + j)
            def _(j=j):
                zback[z] = zout[h, j]

    def stage(h, s):
        if s == 0:
            rs_first(h)
        elif s < far:
            rs_step(h, s, opening=s == 1)
        elif s == far:
            rs_last(h)
            ag_own(h)
        elif s < 2 * far:
            ag_pass(h, s - far, closing=s == 2 * far - 1)
            ag_down(h, s - far)
        else:
            ag_last(h)

    prepare(0)
    spread_tokens(0)
    for h in range(1, GROUPS):
        prepare(h)
    share(0)
    spread_tokens(1)
    for i in range(2):
        loop(0, NZ, lambda k: w_load(i, k).wait())
        loop(0, NZ, lambda k: w_get(i, k).wait_recv())
    select(0)
    stage(0, 0)
    stage(0, 1)
    share(1)
    spread_tokens(2)
    select(1)
    stage(1, 0)
    stage(0, 2)
    stage(1, 1)
    share(2)
    spread_tokens(3)
    stage(0, 3)
    select(2)
    stage(1, 2)
    share(3)
    loop(0, NZ, lambda k: w_load(2, k).wait())
    loop(0, NZ, lambda k: w_get(2, k).wait_recv())
    stage(0, 4)
    stage(2, 0)
    stage(1, 3)
    select(3)
    for t in range(1, 4):
        stage(0, 4 + t)
        stage(2, t)
        stage(1, 3 + t)
        stage(3, t - 1)
    stage(0, 8)
    stage(2, 4)
    stage(1, 7)
    stage(3, 3)
    spread(0)
    stage(2, 5)
    stage(1, 8)
    stage(3, 4)
    spread(1)
    collect(0)
    for s in range(2, far):
        ag_pass(2, s, closing=s == far - 1)
        ag_pass(3, s - 1)
        ag_down(2, s)
        ag_down(3, s - 1)
        if s == 2:
            collect(1)
    ag_last(2)
    ag_pass(3, far - 1, closing=True)
    ag_down(3, far - 1)
    spread(2)
    ag_last(3)
    spread(3)
    collect(2)
    collect(3)
    load[0, 0] = jnp.max(functools.reduce(jnp.maximum, loads)).astype(jnp.int32)

    def b_from(src):
        return remote(
            zout.at[0, 0], zback.at[src], b_send.at[0, 0], b_recv.at[src], (wide, src)
        )

    loop(1, NZ, lambda k: b_from(zs(k)).wait_recv())
    line = []
    for n in range(NZ):
        got = zback[n].astype(F32)
        line += [got[:8, :], got[8:, : block - WIDE_LO]]
    out[...] = jnp.concatenate(line, axis=1).astype(BF16)

    loop(1, NZ, lambda k: z_copy(zs(k)).wait_send())
    for i in range(3):
        loop(0, NZ, lambda k: w_give(i, k).wait_send())
    for h in range(GROUPS):
        loop(1, NX * NY, lambda k: g_copy(h, k).wait_send())
        m_copy(h, cc).wait_send()
        cm_copy(h, 1 - cc).wait_send()
        loop(1, NX * NY, lambda k: r_copy(h, k).wait_send())
        for j in range(2):
            pl.when(z != 2 * h + j)(lambda j=j: b_copy(h, j).wait_send())

    for h in range(GROUPS):
        for d in range(2):
            for s in range(far):
                for p in range(PIECES):
                    if s > 0 or halfway(d, p):
                        rs_sent(h, d, s, p)
                    if s < far - 1 or halfway(d, p):
                        ag_copy(h, d, s, p, z).wait_send()


class Copies:
    def __init__(self, send, recv):
        self.send, self.recv = send, recv
        self.used = 0
        self.started = []

    def slot(self):
        self.used += 1
        return self.used - 1

    def make(self, slot, src, dst, device):
        return pltpu.make_async_remote_copy(
            src_ref=src,
            dst_ref=dst,
            send_sem=self.send.at[slot],
            recv_sem=self.recv.at[slot],
            device_id=device,
            device_id_type=pl.DeviceIdType.MESH,
        )

    def go(self, slot, src, dst, device):
        copy = self.make(slot, src, dst, device)
        copy.start()
        self.started.append(copy)


def every_slot_kernel(
    tok,
    wg_hbm,
    wu_hbm,
    wd_hbm,
    out,
    zin,
    g,
    x,
    sel,
    wcol,
    wg,
    wu,
    wd,
    first,
    part,
    hid,
    acc,
    c,
    core_in,
    ra1,
    ra2,
    rb1,
    rb2,
    zout,
    zback,
    load_sem,
    send,
    recv,
    rs_send,
    rs_recv,
    ag_send,
    ag_recv,
):
    wide, z = lax.axis_index("wide"), lax.axis_index("narrow")
    cc = lax.rem(wide, NC)
    yy = lax.rem(wide // NC, NY)
    xx = wide // (NC * NY)
    block = x.shape[1]
    rows = x.shape[0]
    half = rows // 2
    sub = half // SUBS
    cols = wg.shape[1] // NZ

    def at(px, py, pc):
        return (px * NY + py) * NC + pc

    def xs(k):
        return lax.rem(xx + k, NX)

    def ys(k):
        return lax.rem(yy + k, NY)

    def zs(k):
        return lax.rem(z + k, NZ)

    xdev = {1: (at(xs(1), yy, cc), z), -1: (at(xs(3), yy, cc), z)}
    ydev = {1: (at(xx, ys(1), cc), z), -1: (at(xx, ys(3), cc), z)}
    mate = (at(xx, yy, 1 - cc), z)

    loads = [
        pltpu.make_async_copy(a, b, load_sem.at[i])
        for i, (a, b) in enumerate(((wg_hbm, wg), (wu_hbm, wu), (wd_hbm, wd)))
    ]
    for load in loads:
        load.start()

    barrier = pltpu.get_barrier_semaphore()
    peers = [xdev[1], xdev[-1], ydev[1], ydev[-1], mate] + [(wide, zs(k)) for k in range(1, NZ)]
    for peer in peers:
        pl.semaphore_signal(barrier, inc=1, device_id=peer, device_id_type=pl.DeviceIdType.MESH)
    pl.semaphore_wait(barrier, len(peers))

    copies = Copies(send, recv)

    zslots = {}
    for k in range(1, NZ):
        zslots[k] = copies.slot()
        copies.go(zslots[k], tok.at[zs(k)], zin.at[z], (wide, zs(k)))
    zin[z] = tok[z]
    for k in range(1, NZ):
        src = zs(NZ - k)
        copies.make(zslots[k], tok.at[src], zin.at[src], (wide, src)).wait_recv()
    arrived = zin[...].astype(F32)
    tokens_z = arrived.shape[0] * arrived.shape[1] // 2
    g[xx, yy, cc, :, :WIDE_LO] = arrived[:, :8, :].reshape(tokens_z, WIDE_LO).astype(BF16)
    g[xx, yy, cc, :, WIDE_LO:] = arrived[:, 8:, :].reshape(tokens_z, WIDE_LO).astype(BF16)

    def lane_a(pos):
        return lambda lo, n: g.at[pos, yy, cc, pl.ds(lo, n)]

    def lane_b(pos):
        return lambda lo, n: g.at[xx, pos, cc, pl.ds(32 + lo, n)]

    def plane_a(pos):
        return lambda lo, n: g.at[:, pos, cc, pl.ds(lo, n)]

    def plane_b(pos):
        return lambda lo, n: g.at[pos, :, cc, pl.ds(32 + lo, n)]

    def gather_start(region, step, dev):
        right, left = copies.slot(), copies.slot()
        own = region(step(0))(0, 32)
        copies.go(right, own, own, dev[1])
        copies.go(left, own, own, dev[-1])
        return right, left

    def gather_forward(region, step, dev, slots):
        right, left = copies.slot(), copies.slot()
        before, after = region(step(3)), region(step(1))
        copies.make(slots[0], before(0, 32), before(0, 32), dev[-1]).wait_recv()
        copies.go(right, before(0, 16), before(0, 16), dev[1])
        copies.make(slots[1], after(0, 32), after(0, 32), dev[1]).wait_recv()
        copies.go(left, after(16, 16), after(16, 16), dev[-1])
        return right, left

    def gather_end(region, step, dev, slots):
        far = region(step(2))
        copies.make(slots[0], far(0, 16), far(0, 16), dev[-1]).wait_recv()
        copies.make(slots[1], far(16, 16), far(16, 16), dev[1]).wait_recv()

    core_waits = []

    def to_mate(region, step, k):
        slot = copies.slot()
        copies.go(slot, region(step(k))(0, 32), region(step(k))(0, 32), mate)
        core_waits.append((slot, region, step, k))

    a1 = gather_start(lane_a, xs, xdev)
    b1 = gather_start(lane_b, ys, ydev)
    a2 = gather_forward(lane_a, xs, xdev, a1)
    b2 = gather_forward(lane_b, ys, ydev, b1)
    gather_end(lane_a, xs, xdev, a2)
    a3 = gather_start(plane_a, ys, ydev)
    gather_end(lane_b, ys, ydev, b2)
    b3 = gather_start(plane_b, xs, xdev)
    to_mate(plane_a, ys, 0)
    to_mate(plane_b, xs, 0)
    a4 = gather_forward(plane_a, ys, ydev, a3)
    b4 = gather_forward(plane_b, xs, xdev, b3)
    for k in (1, 3):
        to_mate(plane_a, ys, k)
        to_mate(plane_b, xs, k)
    gather_end(plane_a, ys, ydev, a4)
    to_mate(plane_a, ys, 2)
    gather_end(plane_b, xs, xdev, b4)
    to_mate(plane_b, xs, 2)
    other = {
        plane_a: lambda pos: g.at[:, pos, 1 - cc, pl.ds(0, 32)],
        plane_b: lambda pos: g.at[pos, :, 1 - cc, pl.ds(32, 32)],
    }
    for slot, region, step, k in core_waits:
        there = other[region](step(k))
        copies.make(slot, there, there, mate).wait_recv()

    batches = 8
    toks = NX * NY * NC * 64 // batches
    slots = rows // batches
    devs = slots // 4
    lane = lax.broadcasted_iota(jnp.int32, (toks, SIDE), 1)
    row = lax.broadcasted_iota(jnp.int32, (toks, SIDE), 0)
    mine = (lax.rem(lane, 32) == wide) & (lane < 96)
    square_r = lax.broadcasted_iota(jnp.int32, (toks, toks), 0)
    square_c = lax.broadcasted_iota(jnp.int32, (toks, toks), 1)
    lower = ((square_r // 8 == square_c // 8) & (square_c < square_r)).astype(F32).astype(BF16)
    for b in range(batches):
        here = g[b // 2, 2 * (b % 2) : 2 * (b % 2) + 2].reshape(toks, block + SIDE)
        weight = jnp.sum(
            jnp.where(mine, here[:, block:].astype(F32), 0.0), axis=1, keepdims=True
        )
        weight = jnp.broadcast_to(weight, (toks, SIDE))
        chosen = jnp.where(weight > 0.0, 1.0, 0.0)
        rank = dot(lower, chosen.astype(BF16)).astype(jnp.int32)
        place = rank * devs + row // 8
        pick = jnp.where((lane == place) & (weight > 0.0), 1.0, 0.0).astype(BF16)
        sel[b] = pick
        wcol[b] = weight
        taken = lax.dot_general(
            pick, here[:, :block], (((0,), (0,)), ((), ())), preferred_element_type=F32
        )
        x[b * slots : (b + 1) * slots, :] = taken.astype(BF16)

    loads[0].wait()
    loads[1].wait()
    zdev = ((wide, zs(1)), (wide, zs(NZ - 1)))

    def ring(s, d):
        return lax.rem(z + NZ - s, NZ) if d == 0 else lax.rem(z + s, NZ)

    def product(d, q, chunk):
        rows_here = x[pl.ds(pl.multiple_of(d * half + q * sub, sub), sub), :]
        at_cols = pl.ds(pl.multiple_of(chunk * cols, cols), cols)
        return dot(rows_here, wg[:, at_cols]), dot(rows_here, wu[:, at_cols])

    def rs_copy(d, s, q, src):
        return pltpu.make_async_remote_copy(
            src_ref=src,
            dst_ref=part.at[d, s, q],
            send_sem=rs_send.at[d, s, q],
            recv_sem=rs_recv.at[d, s, q],
            device_id=zdev[d],
            device_id_type=pl.DeviceIdType.MESH,
        )

    def ag_copy(d, s, q, chunk):
        here = hid.at[chunk, pl.ds(pl.multiple_of(d * half + q * sub, sub), sub)]
        return pltpu.make_async_remote_copy(
            src_ref=here,
            dst_ref=here,
            send_sem=ag_send.at[d, s, q],
            recv_sem=ag_recv.at[d, s, q],
            device_id=zdev[d],
            device_id_type=pl.DeviceIdType.MESH,
        )

    def each_sub(body):
        def step(q, carry):
            for d in range(2):
                body(d, q)
            return carry

        lax.fori_loop(0, SUBS, step, 0)

    def rs_first(d, q):
        gate, up = product(d, q, ring(1, d))
        first[d, q, :, :cols] = gate.astype(BF16)
        first[d, q, :, cols:] = up.astype(BF16)
        rs_copy(d, 0, q, first.at[d, q]).start()

    each_sub(rs_first)

    def rs_step(s, carry):
        def body(d, q):
            gate, up = product(d, q, ring(s + 1, d))
            rs_copy(d, s - 1, q, first.at[d, q]).wait_recv()
            here = part.at[d, s - 1, q]
            here[:, :cols] = (here[:, :cols].astype(F32) + gate).astype(BF16)
            here[:, cols:] = (here[:, cols:].astype(F32) + up).astype(BF16)
            rs_copy(d, s, q, here).start()

        each_sub(body)
        return carry

    lax.fori_loop(1, NZ - 1, rs_step, 0)
    loads[2].wait()

    def down(d, q, chunk):
        at_rows = pl.ds(pl.multiple_of(d * half + q * sub, sub), sub)
        at_cols = pl.ds(pl.multiple_of(chunk * cols, cols), cols)
        return at_rows, dot(hid[chunk, at_rows, :], wd[at_cols, :])

    def rs_last(d, q):
        gate, up = product(d, q, z)
        rs_copy(d, NZ - 2, q, first.at[d, q]).wait_recv()
        here = part.at[d, NZ - 2, q]
        gate = gate + here[:, :cols].astype(F32)
        up = up + here[:, cols:].astype(F32)
        hidden = gate / (1.0 + jnp.exp(-gate)) * up
        at_rows = pl.ds(pl.multiple_of(d * half + q * sub, sub), sub)
        hid[z, at_rows, :] = hidden.astype(BF16)
        ag_copy(d, 0, q, z).start()
        at_rows, value = down(d, q, z)
        acc[at_rows, :] = value

    each_sub(rs_last)

    def ag_step(s, carry):
        def body(d, q):
            chunk = ring(s, d)
            ag_copy(d, s - 1, q, chunk).wait_recv()
            ag_copy(d, s, q, chunk).start()
            at_rows, value = down(d, q, chunk)
            acc[at_rows, :] = acc[at_rows, :] + value

        each_sub(body)
        return carry

    lax.fori_loop(1, NZ - 1, ag_step, 0)

    core_slots = [copies.slot() for _ in range(NX)]
    for b in range(batches):
        d, q = b // SUBS, b % SUBS
        chunk = ring(NZ - 1, d)
        ag_copy(d, NZ - 2, q, chunk).wait_recv()
        at_rows, value = down(d, q, chunk)
        expert_out = (acc[at_rows, :] + value).astype(BF16)
        mixed = dot(sel[b], expert_out) * wcol[b][:, :1]
        c[b // 2, 2 * (b % 2) : 2 * (b % 2) + 2] = mixed.astype(BF16).reshape(2, NC, 64, block)
        if b % 2 == 1:
            copies.go(core_slots[b // 2], c.at[b // 2, :, 1 - cc], core_in.at[b // 2], mate)
    for px in range(NX):
        copies.make(core_slots[px], c.at[px, :, cc], core_in.at[px], mate).wait_recv()
        c[px, :, cc] = (c[px, :, cc].astype(F32) + core_in[px].astype(F32)).astype(BF16)

    def c_plane_a(pos, lo, n):
        return c.at[:, pos, cc, pl.ds(lo, n)]

    def c_plane_b(pos, lo, n):
        return c.at[pos, :, cc, pl.ds(32 + lo, n)]

    def c_lane_a(pos, lo, n):
        return c.at[pos, yy, cc, pl.ds(lo, n)]

    def c_lane_b(pos, lo, n):
        return c.at[xx, pos, cc, pl.ds(32 + lo, n)]

    def add_into(ref, other_ref):
        ref[...] = (ref[...].astype(F32) + other_ref[...].astype(F32)).astype(BF16)

    def scatter_start(region, step, dev, buf):
        right, left = copies.slot(), copies.slot()
        copies.go(right, region(step(2), 0, 16), buf.at[0], dev[1])
        copies.go(left, region(step(2), 16, 16), buf.at[1], dev[-1])
        return right, left

    def scatter_forward(region, step, dev, buf, buf2, slots):
        right, left = copies.slot(), copies.slot()
        copies.make(slots[0], region(step(2), 0, 16), buf.at[0], dev[-1]).wait_recv()
        add_into(region(step(1), 0, 16), buf.at[0])
        copies.go(right, region(step(1), 0, 32), buf2.at[0], dev[1])
        copies.make(slots[1], region(step(2), 16, 16), buf.at[1], dev[1]).wait_recv()
        add_into(region(step(3), 16, 16), buf.at[1])
        copies.go(left, region(step(3), 0, 32), buf2.at[1], dev[-1])
        return right, left

    def scatter_end(region, step, dev, buf2, slots):
        copies.make(slots[0], region(step(0), 0, 32), buf2.at[0], dev[-1]).wait_recv()
        copies.make(slots[1], region(step(0), 0, 32), buf2.at[1], dev[1]).wait_recv()
        here = region(step(0), 0, 32)
        return here[...].astype(F32) + buf2[0].astype(F32) + buf2[1].astype(F32)

    a1 = scatter_start(c_plane_a, ys, ydev, ra1.at[0])
    b1 = scatter_start(c_plane_b, xs, xdev, ra1.at[1])
    a2 = scatter_forward(c_plane_a, ys, ydev, ra1.at[0], ra2.at[0], a1)
    b2 = scatter_forward(c_plane_b, xs, xdev, ra1.at[1], ra2.at[1], b1)
    total = scatter_end(c_plane_a, ys, ydev, ra2.at[0], a2)
    c[:, yy, cc, :32, :] = total.astype(BF16)
    a3 = scatter_start(c_lane_a, xs, xdev, rb1.at[0])
    total = scatter_end(c_plane_b, xs, xdev, ra2.at[1], b2)
    c[xx, :, cc, 32:, :] = total.astype(BF16)
    b3 = scatter_start(c_lane_b, ys, ydev, rb1.at[1])
    a4 = scatter_forward(c_lane_a, xs, xdev, rb1.at[0], rb2.at[0], a3)
    b4 = scatter_forward(c_lane_b, ys, ydev, rb1.at[1], rb2.at[1], b3)
    sums = [
        scatter_end(c_lane_a, xs, xdev, rb2.at[0], a4),
        scatter_end(c_lane_b, ys, ydev, rb2.at[1], b4),
    ]

    for i, total in enumerate(sums):
        lo = total[:, :WIDE_LO].reshape(4, 8, WIDE_LO)
        hi = total[:, WIDE_LO:].reshape(4, 8, block - WIDE_LO)
        hi = jnp.concatenate([hi, jnp.zeros((4, 8, 2 * WIDE_LO - block), F32)], axis=2)
        zout[4 * i : 4 * i + 4] = jnp.concatenate([lo, hi], axis=1).astype(BF16)
    zslots = {}
    for k in range(1, NZ):
        zslots[k] = copies.slot()
        copies.go(zslots[k], zout.at[zs(k)], zback.at[z], (wide, zs(k)))
    zback[z] = zout[z]
    for k in range(1, NZ):
        src = zs(NZ - k)
        copies.make(zslots[k], zout.at[src], zback.at[src], (wide, src)).wait_recv()
    pieces = []
    for n in range(NZ):
        got = zback[n].astype(F32)
        pieces += [got[:8, :], got[8:, : block - WIDE_LO]]
    out[...] = jnp.concatenate(pieces, axis=1).astype(BF16)

    for copy in copies.started:
        copy.wait_send()

    def drain(s, carry):
        def body(d, q):
            rs_copy(d, s, q, first.at[d, q]).wait_send()
            ag_copy(d, s, q, ring(s, d)).wait_send()

        each_sub(body)
        return carry

    lax.fori_loop(0, NZ - 1, drain, 0)


def every_slot(tok_rows, width, capacity, tok, w_gate, w_up, w_down):
    block, ff = w_gate.shape
    rows = NX * NY * NC * NZ * 2 * capacity
    half = rows // 2
    sub = half // SUBS
    cols = ff // NZ
    vmem = pl.BlockSpec(memory_space=pltpu.VMEM)
    hbm = pl.BlockSpec(memory_space=pl.ANY)
    line = block + SIDE
    copies = 7 + 24 + 4 + 16 + 7
    return pl.pallas_call(
        every_slot_kernel,
        out_shape=jax.ShapeDtypeStruct((tok_rows, width), BF16),
        in_specs=[vmem, hbm, hbm, hbm],
        out_specs=vmem,
        scratch_shapes=[
            pltpu.VMEM((NZ, 16, WIDE_LO), BF16),
            pltpu.VMEM((NX, NY, NC, 64, line), BF16),
            pltpu.VMEM((rows, block), BF16),
            pltpu.VMEM((8, 256, SIDE), BF16),
            pltpu.VMEM((8, 256, SIDE), F32),
            pltpu.VMEM((block, ff), BF16),
            pltpu.VMEM((block, ff), BF16),
            pltpu.VMEM((ff, block), BF16),
            pltpu.VMEM((2, SUBS, sub, 2 * cols), BF16),
            pltpu.VMEM((2, NZ - 1, SUBS, sub, 2 * cols), BF16),
            pltpu.VMEM((NZ, rows, cols), BF16),
            pltpu.VMEM((rows, block), F32),
            pltpu.VMEM((NX, NY, NC, 64, block), BF16),
            pltpu.VMEM((NX, NY, 64, block), BF16),
            pltpu.VMEM((2, 2, 4, 16, block), BF16),
            pltpu.VMEM((2, 2, 4, 32, block), BF16),
            pltpu.VMEM((2, 2, 16, block), BF16),
            pltpu.VMEM((2, 2, 32, block), BF16),
            pltpu.VMEM((NZ, 16, WIDE_LO), BF16),
            pltpu.VMEM((NZ, 16, WIDE_LO), BF16),
            pltpu.SemaphoreType.DMA((3,)),
            pltpu.SemaphoreType.DMA((copies,)),
            pltpu.SemaphoreType.DMA((copies,)),
            pltpu.SemaphoreType.DMA((2, NZ - 1, SUBS)),
            pltpu.SemaphoreType.DMA((2, NZ - 1, SUBS)),
            pltpu.SemaphoreType.DMA((2, NZ - 1, SUBS)),
            pltpu.SemaphoreType.DMA((2, NZ - 1, SUBS)),
        ],
        compiler_params=pltpu.CompilerParams(
            collective_id=1, has_side_effects=True, vmem_limit_bytes=58 * 1024 * 1024
        ),
        cost_estimate=pl.CostEstimate(
            flops=6 * rows * block * ff, bytes_accessed=6 * block * ff, transcendentals=rows * cols
        ),
        name="every_slot",
    )(tok, w_gate, w_up, w_down)


def on_device(tokens, routes, gates, fallback, w_gate, w_up, w_down):
    experts = lax.axis_size("wide")
    tok_rows, width = tokens.shape
    capacity = min(tok_rows // 2, tok_rows * routes.shape[1] // experts)
    weights = (w_gate[0], w_up[0], w_down[0])
    mixed, tok, load = packed(capacity, tokens, routes, gates, fallback[None, :], *weights)
    return lax.cond(
        load[0, 0] > ROWS,
        lambda: every_slot(tok_rows, width, capacity, tok, *weights),
        lambda: mixed,
    )


def packed(capacity, tokens, routes, gates, fallback, w_gate, w_up, w_down):
    block, ff = w_gate.shape
    tok_rows, width = tokens.shape
    cols = ff // NC // NZ
    vmem = pl.BlockSpec(memory_space=pltpu.VMEM)
    hbm = pl.BlockSpec(memory_space=pl.ANY)
    line = block + SIDE
    dma = pltpu.SemaphoreType.DMA
    half = BOUNDS[PIECES // 2]
    return pl.pallas_call(
        functools.partial(kernel, capacity),
        out_shape=(
            jax.ShapeDtypeStruct((tok_rows, width), BF16),
            jax.ShapeDtypeStruct((NZ, 16, WIDE_LO), BF16),
            jax.ShapeDtypeStruct((1, 1), jnp.int32),
        ),
        in_specs=[vmem] * 4 + [hbm] * 3,
        out_specs=(vmem, vmem, pl.BlockSpec(memory_space=pltpu.SMEM)),
        scratch_shapes=[
            pltpu.VMEM((NZ, 16, WIDE_LO), BF16),
            pltpu.VMEM((NX, NY, NC, 64, line), BF16),
            pltpu.VMEM((GROUPS, ROWS, 2 * block), BF16),
            pltpu.VMEM((GROUPS, 512, ROWS), BF16),
            pltpu.VMEM((GROUPS, ROWS, SIDE), F32),
            pltpu.VMEM((GROUPS, ROWS, SIDE), BF16),
            pltpu.VMEM((NZ, 2 * block, 2 * cols), BF16),
            pltpu.VMEM((NZ, 2 * cols, block), BF16),
            pltpu.VMEM((GROUPS, 2, half, 2 * cols), BF16),
            pltpu.VMEM((GROUPS, 2, NZ // 2, ROWS, 2 * cols), BF16),
            pltpu.VMEM((NZ, GROUPS, ROWS, cols), BF16),
            pltpu.VMEM((2, ROWS, block), F32),
            pltpu.VMEM((GROUPS, NX, NY, NC, 16, block), BF16),
            pltpu.VMEM((GROUPS, NX, NY, 16, block), BF16),
            pltpu.VMEM((GROUPS, NX, NY, 16, block), BF16),
            pltpu.VMEM((GROUPS, 2, 16, WIDE_LO), BF16),
            pltpu.VMEM((NZ, 16, WIDE_LO), BF16),
            dma((3, NZ)),
            dma((3, NZ)),
            dma((3, NZ)),
            dma((NZ,)),
            dma((NZ,)),
            dma((GROUPS, NX * NY)),
            dma((GROUPS, NX * NY)),
            dma((GROUPS,)),
            dma((GROUPS,)),
            dma((GROUPS, 2, NZ // 2, PIECES)),
            dma((GROUPS, 2, NZ // 2, PIECES)),
            dma((GROUPS, 2, NZ // 2, PIECES)),
            dma((GROUPS, 2, NZ // 2, PIECES)),
            dma((GROUPS,)),
            dma((GROUPS,)),
            dma((GROUPS, NX * NY)),
            dma((GROUPS, NX * NY)),
            dma((GROUPS, 2)),
            dma((NZ,)),
        ],
        compiler_params=pltpu.CompilerParams(
            collective_id=0, has_side_effects=True, vmem_limit_bytes=60 * 1024 * 1024
        ),
        cost_estimate=pl.CostEstimate(
            flops=6 * GROUPS * ROWS * block * ff,
            bytes_accessed=6 * block * ff,
            transcendentals=GROUPS * ROWS * cols,
        ),
        name="packed",
    )(tokens, routes, gates, fallback, w_gate, w_up, w_down)


def solution(mesh):
    placed = (
        P(("wide", "narrow"), None),
        P(("wide", "narrow"), None),
        P(("wide", "narrow"), None),
        P(),
        P("wide", "narrow", None),
        P("wide", "narrow", None),
        P("wide", None, "narrow"),
    )
    return jax.shard_map(
        on_device,
        mesh=mesh,
        in_specs=placed,
        out_specs=P(("wide", "narrow"), None),
        check_vma=False,
    )
```

```python
import functools

import jax
import jax.numpy as jnp
from jax import lax
from jax.experimental import pallas as pl
from jax.experimental.pallas import tpu as pltpu
from jax.sharding import PartitionSpec as P

F32 = jnp.float32
BF16 = jnp.bfloat16
NX, NY, NC, NZ = 4, 4, 2, 8
SIDE = 128
WIDE_LO = 512
GROUPS = 4
PIECES = 2
SUBS = 4
BOUNDS = (0, 208, 400)
ROWS = BOUNDS[-1]


def dot(a, b):
    return jnp.dot(a, b, preferred_element_type=F32)


def make_rows(capacity, tokens, routes, gates, fallback, tok):
    tok_rows, chosen_count = routes.shape
    experts = fallback.shape[1]
    lane = lax.broadcasted_iota(jnp.int32, (tok_rows, experts), 1)
    row = lax.broadcasted_iota(jnp.int32, (tok_rows, experts), 0)
    hits = jnp.zeros((tok_rows, experts), F32)
    weight_of = jnp.zeros((tok_rows, experts), F32)
    for k in range(chosen_count):
        named = routes[:, k : k + 1] == lane
        hits = hits + jnp.where(named, 1.0, 0.0)
        weight_of = weight_of + jnp.where(named, gates[:, k : k + 1], 0.0)
    ranks = jnp.zeros((tok_rows, experts), F32)
    for t in range(tok_rows - 1):
        ranks = ranks + jnp.where(row > t, hits[t : t + 1, :], 0.0)
    primary = jnp.where(ranks < capacity, weight_of, 0.0)
    to = lax.broadcasted_iota(jnp.int32, (experts, experts), 0)
    redirect = jnp.where(to == fallback[...], 1.0, 0.0).astype(BF16)

    def split(value):
        terms = []
        for _ in range(3):
            terms.append(value.astype(BF16))
            value = value - terms[-1].astype(F32)
        return terms

    weights = primary
    for term in split(weight_of - primary):
        weights = weights + lax.dot_general(
            term, redirect, (((1,), (1,)), ((), ())), preferred_element_type=F32
        )
    terms = [term.astype(F32) for term in split(weights)]
    side = jnp.concatenate(terms + [jnp.zeros_like(weights)], axis=1)
    width = tokens.shape[1]
    block = width // NZ
    for n in range(NZ):
        here = tokens[:, n * block : (n + 1) * block].astype(F32)
        tail = jnp.concatenate([here[:, WIDE_LO:], side], axis=1)
        tok[n] = jnp.concatenate([here[:, :WIDE_LO], tail], axis=0).astype(BF16)


def kernel(
    capacity,
    tokens,
    routes,
    gates,
    fallback,
    wg_hbm,
    wu_hbm,
    wd_hbm,
    out,
    tok,
    load,
    zin,
    g,
    x,
    sel,
    wrow,
    own0,
    w1,
    w2,
    first,
    part,
    hid,
    acc,
    c,
    core_in,
    land,
    zout,
    zback,
    wl,
    ws,
    wr,
    z_send,
    z_recv,
    g_send,
    g_recv,
    m_send,
    m_recv,
    rs_send,
    rs_recv,
    ag_send,
    ag_recv,
    cm_send,
    cm_recv,
    r_send,
    r_recv,
    b_send,
    b_recv,
):
    wide, z = lax.axis_index("wide"), lax.axis_index("narrow")
    cc = lax.rem(wide, NC)
    yy = lax.rem(wide // NC, NY)
    xx = wide // (NC * NY)
    block = x.shape[2] // 2
    rows = x.shape[1]
    cols = w1.shape[2] // 2
    part_ff = NZ * cols
    side = g.shape[4] - block

    def at(px, py, pc):
        return (px * NY + py) * NC + pc

    def zs(k):
        return lax.rem(z + k, NZ)

    def chip(k):
        return lax.rem(xx + k // NY, NX), lax.rem(yy + lax.rem(k, NY), NY)

    def chip_back(k):
        return lax.rem(xx + NX - k // NY, NX), lax.rem(yy + NY - lax.rem(k, NY), NY)

    mate = (at(xx, yy, 1 - cc), z)

    def remote(src, dst, send, recv, device):
        return pltpu.make_async_remote_copy(
            src_ref=src,
            dst_ref=dst,
            send_sem=send,
            recv_sem=recv,
            device_id=device,
            device_id_type=pl.DeviceIdType.MESH,
        )

    def loop(lo, hi, body):
        def step(i, carry):
            body(i)
            return carry

        lax.fori_loop(lo, hi, step, 0)

    def w_refs(i, k, half, owner):
        lanes = pl.ds(pl.multiple_of(half * part_ff + k * cols, cols), cols)
        deep = pl.ds(pl.multiple_of(owner * block, block), block)
        if i < 2:
            src = (wg_hbm, wu_hbm)[i].at[:, lanes]
            return src, w1.at[k, deep, pl.ds(i * cols, cols)]
        return wd_hbm.at[lanes, :], w2.at[k, pl.ds(pl.multiple_of(owner * cols, cols), cols)]

    def w_load(i, k):
        src, dst = w_refs(i, k, cc, cc)
        return pltpu.make_async_copy(src, dst, wl.at[i, k])

    def w_give(i, k):
        src, dst = w_refs(i, k, 1 - cc, cc)
        return remote(src, dst, ws.at[i, k], wr.at[i, k], mate)

    def w_get(i, k):
        src, dst = w_refs(i, k, cc, 1 - cc)
        return remote(src, dst, ws.at[i, k], wr.at[i, k], mate)

    for i in range(3):
        loop(0, NZ, lambda k: w_load(i, k).start())

    make_rows(capacity, tokens, routes, gates, fallback, tok)

    barrier = pltpu.get_barrier_semaphore()

    def greet(device):
        pl.semaphore_signal(barrier, inc=1, device_id=device, device_id_type=pl.DeviceIdType.MESH)

    for k in range(1, NZ):
        greet((wide, zs(k)))
    greet(mate)
    loop(1, NX * NY, lambda k: greet((at(*chip(k), cc), z)))
    pl.semaphore_wait(barrier, NZ - 1 + 1 + NX * NY - 1)

    def z_copy(to):
        return remote(tok.at[to], zin.at[z], z_send.at[to], z_recv.at[z], (wide, to))

    def z_from(src):
        return remote(tok.at[src], zin.at[src], z_send.at[src], z_recv.at[src], (wide, src))

    loop(1, NZ, lambda k: z_copy(zs(k)).start())
    zin[z] = tok[z]
    for i in range(3):
        loop(0, NZ, lambda k: w_give(i, k).start())

    def group_rows(h):
        return pl.ds(16 * h, 16)

    def g_copy(h, k):
        px, py = chip(k)
        here = g.at[xx, yy, cc, group_rows(h)]
        return remote(here, here, g_send.at[h, k], g_recv.at[h, k], (at(px, py, cc), z))

    def g_from(h, k):
        px, py = chip_back(k)
        there = g.at[px, py, cc, group_rows(h)]
        return remote(there, there, g_send.at[h, k], g_recv.at[h, k], (at(px, py, cc), z))

    def prepare(h):
        for src in (2 * h, 2 * h + 1):
            pl.when(z != src)(lambda src=src: z_from(src).wait_recv())
        arrived = zin[2 * h : 2 * h + 2].astype(F32)
        for half in range(2):
            lanes = slice(half * WIDE_LO, (half + 1) * WIDE_LO)
            value = arrived[:, 8 * half : 8 * half + 8, :].reshape(16, WIDE_LO)
            g[xx, yy, cc, 16 * h : 16 * h + 16, lanes] = value.astype(BF16)

    def spread_tokens(h):
        loop(1, NX * NY, lambda k: g_copy(h, k).start())

    def m_copy(h, core):
        here = g.at[:, :, core, group_rows(h)]
        return remote(here, here, m_send.at[h], m_recv.at[h], mate)

    def share(h):
        loop(1, NX * NY, lambda k: g_from(h, k).wait_recv())
        m_copy(h, cc).start()

    toks = 512
    expert0 = wide - cc

    loads = []

    def select(h):
        m_copy(h, 1 - cc).wait_recv()
        here = g[:, :, :, 16 * h : 16 * h + 16].reshape(toks, block + side)
        weights = here[:, block:].astype(F32)
        lane = lax.broadcasted_iota(jnp.int32, (toks, side), 1)

        def weight_of(expert):
            mine = (lax.rem(lane, 32) == expert) & (lane < 96)
            return jnp.sum(jnp.where(mine, weights, 0.0), axis=1, keepdims=True)

        chosen = [jnp.where(weight_of(expert0 + j) > 0.0, 1.0, 0.0) for j in range(2)]
        both = jnp.where(lane < side // 2, chosen[0], chosen[1]).astype(BF16)
        square_r = lax.broadcasted_iota(jnp.int32, (toks, toks), 0)
        square_c = lax.broadcasted_iota(jnp.int32, (toks, toks), 1)
        lower = jnp.where(square_c < square_r, 1.0, 0.0).astype(BF16)
        before = dot(lower, both)
        total0 = jnp.sum(chosen[0], axis=0, keepdims=True)
        place0 = jnp.where(chosen[0] > 0.0, before[:, :1], -1.0).astype(jnp.int32)
        place1 = jnp.where(chosen[1] > 0.0, before[:, side // 2 : side // 2 + 1] + total0, -1.0)
        place1 = place1.astype(jnp.int32)
        slot = lax.broadcasted_iota(jnp.int32, (toks, rows), 1)
        pick = jnp.where((slot == place0) | (slot == place1), 1.0, 0.0).astype(BF16)
        sel[h] = pick
        taken = lax.dot_general(pick, here, (((0,), (0,)), ((), ())), preferred_element_type=F32)
        row = lax.broadcasted_iota(jnp.int32, (rows, side), 0)
        lane = lax.broadcasted_iota(jnp.int32, (rows, side), 1)
        is0 = row < total0.astype(jnp.int32)
        own0[h] = jnp.where(is0, 1.0, 0.0).astype(BF16)
        mine = (lax.rem(lane, 32) == jnp.where(is0, expert0, expert0 + 1)) & (lane < 96)
        weight = jnp.sum(jnp.where(mine, taken[:, block:], 0.0), axis=1, keepdims=True)
        wrow[h] = jnp.broadcast_to(weight, (rows, side))
        first0 = is0[:, :1]
        x[h, :, :block] = jnp.where(first0, taken[:, :block], 0.0).astype(BF16)
        x[h, :, block:] = jnp.where(first0, 0.0, taken[:, :block]).astype(BF16)

        pair_r = lax.broadcasted_iota(jnp.int32, (side, side), 0)
        pair_c = lax.broadcasted_iota(jnp.int32, (side, side), 1)
        pair = jnp.where((pair_r < 32) & (pair_r // 2 == pair_c // 2), 1.0, 0.0).astype(BF16)
        any_chip = dot(jnp.where(weights > 0.0, 1.0, 0.0).astype(BF16), pair)
        count = jnp.broadcast_to(jnp.sum(any_chip, axis=0, keepdims=True), (8, side))
        loads.append(count)

    far = NZ // 2
    zdev = ((wide, zs(1)), (wide, zs(NZ - 1)))

    def rows_of(p):
        return pl.ds(BOUNDS[p], BOUNDS[p + 1] - BOUNDS[p])

    def halfway(d, p):
        return p // (PIECES // 2) == d

    def ring(s, d):
        return lax.rem(z + NZ - s, NZ) if d == 0 else lax.rem(z + s, NZ)

    def product(h, here, chunk):
        return dot(x[h, here, :], w1[chunk])

    def rs_copy(h, d, s, p):
        src = first.at[h, d, pl.ds(BOUNDS[p] - BOUNDS[d * (PIECES // 2)], BOUNDS[p + 1] - BOUNDS[p])] if s == 0 else part.at[h, d, s - 1, rows_of(p)]
        return remote(
            src,
            part.at[h, d, s, rows_of(p)],
            rs_send.at[h, d, s, p],
            rs_recv.at[h, d, s, p],
            zdev[d],
        )

    def rs_wait(h, d, s, p):
        here = part.at[h, d, s, rows_of(p)]
        remote(here, here, rs_send.at[h, d, s, p], rs_recv.at[h, d, s, p], zdev[d]).wait_recv()

    def rs_sent(h, d, s, p):
        here = part.at[h, d, s, rows_of(p)]
        remote(here, here, rs_send.at[h, d, s, p], rs_recv.at[h, d, s, p], zdev[d]).wait_send()

    def ag_copy(h, d, s, p, chunk):
        here = hid.at[chunk, h, rows_of(p)]
        return remote(here, here, ag_send.at[h, d, s, p], ag_recv.at[h, d, s, p], zdev[d])

    def rs_first(h):
        for d in range(2):
            lo, hi = BOUNDS[d * (PIECES // 2)], BOUNDS[(d + 1) * (PIECES // 2)]
            value = product(h, slice(lo, hi), ring(far, d))
            first[h, d, : hi - lo, :] = value.astype(BF16)
            for p in range(PIECES):
                if halfway(d, p):
                    rs_copy(h, d, 0, p).start()

    def rs_step(h, s, opening=False):
        for d in range(2):
            value = product(h, slice(None), ring(NZ - far + s, d))
            for p in sorted(range(PIECES), key=lambda p: opening and halfway(d, p)):
                own = value[BOUNDS[p] : BOUNDS[p + 1]]
                here = part.at[h, d, s - 1, rows_of(p)]
                if opening and not halfway(d, p):
                    here[...] = own.astype(BF16)
                else:
                    rs_wait(h, d, s - 1, p)
                    here[...] = (here[...].astype(F32) + own).astype(BF16)
                rs_copy(h, d, s, p).start()

    def down(h, chunk):
        hidden = hid[chunk, h].astype(F32)
        mask = own0[h].astype(F32)
        apart = jnp.concatenate([hidden * mask, hidden * (1.0 - mask)], axis=1)
        return dot(apart.astype(BF16), w2[chunk])

    def rs_last(h):
        value = product(h, slice(None), z)
        for p in range(PIECES):
            total = value[BOUNDS[p] : BOUNDS[p + 1]]
            for d in range(2):
                rs_wait(h, d, far - 1, p)
                total = total + part[h, d, far - 1, rows_of(p), :].astype(F32)
            gate, up = total[:, :cols], total[:, cols:]
            hid[z, h, rows_of(p), :] = (gate / (1.0 + jnp.exp(-gate)) * up).astype(BF16)
            for d in range(2):
                ag_copy(h, d, 0, p, z).start()

    def ag_own(h):
        acc[h % 2] = down(h, z)

    def ag_pass(h, s, closing=False):
        for p in range(PIECES):
            for d in range(2):
                ag_copy(h, d, s - 1, p, ring(s, d)).wait_recv()
                if not closing or halfway(d, p):
                    ag_copy(h, d, s, p, ring(s, d)).start()

    def ag_down(h, s):
        acc[h % 2] = acc[h % 2] + down(h, ring(s, 0)) + down(h, ring(s, 1))

    def cm_copy(h, core):
        return remote(c.at[h, :, :, core], core_in.at[h], cm_send.at[h], cm_recv.at[h], mate)

    def ag_last(h):
        for p in range(PIECES):
            for d in range(2):
                if halfway(d, p):
                    ag_copy(h, d, far - 1, p, ring(far, d)).wait_recv()
        weighted = (acc[h % 2] + down(h, ring(far, 0))) * wrow[h][:, :1]
        mixed = dot(sel[h], weighted.astype(BF16))
        c[h] = mixed.astype(BF16).reshape(NX, NY, NC, 16, block)
        cm_copy(h, 1 - cc).start()

    def r_copy(h, k):
        px, py = chip(k)
        return remote(
            c.at[h, px, py, cc],
            land.at[h, xx, yy],
            r_send.at[h, k],
            r_recv.at[h, k],
            (at(px, py, cc), z),
        )

    def r_from(h, k):
        px, py = chip_back(k)
        return remote(
            c.at[h, px, py, cc],
            land.at[h, px, py],
            r_send.at[h, k],
            r_recv.at[h, k],
            (at(px, py, cc), z),
        )

    def spread(h):
        cm_copy(h, cc).wait_recv()
        for px in range(NX):
            both = c[h, px, :, cc].astype(F32) + core_in[h, px].astype(F32)
            c[h, px, :, cc] = both.astype(BF16)
        land[h, xx, yy] = c[h, xx, yy, cc]
        loop(1, NX * NY, lambda k: r_copy(h, k).start())

    def b_copy(h, j):
        to = 2 * h + j
        return remote(zout.at[h, j], zback.at[z], b_send.at[h, j], b_recv.at[z], (wide, to))

    def collect(h):
        loop(1, NX * NY, lambda k: r_from(h, k).wait_recv())
        total = jnp.sum(land[h].reshape(NX * NY, 16, block).astype(F32), axis=0)
        lo = total[:, :WIDE_LO].reshape(2, 8, WIDE_LO)
        hi = total[:, WIDE_LO:].reshape(2, 8, block - WIDE_LO)
        hi = jnp.concatenate([hi, jnp.zeros((2, 8, 2 * WIDE_LO - block), F32)], axis=2)
        zout[h] = jnp.concatenate([lo, hi], axis=1).astype(BF16)
        for j in range(2):
            pl.when(z != 2 * h + j)(lambda j=j: b_copy(h, j).start())

            @pl.when(z == 2 * h + j)
            def _(j=j):
                zback[z] = zout[h, j]

    def stage(h, s):
        if s == 0:
            rs_first(h)
        elif s < far:
            rs_step(h, s, opening=s == 1)
        elif s == far:
            rs_last(h)
            ag_own(h)
        elif s < 2 * far:
            ag_pass(h, s - far, closing=s == 2 * far - 1)
            ag_down(h, s - far)
        else:
            ag_last(h)

    prepare(0)
    spread_tokens(0)
    for h in range(1, GROUPS):
        prepare(h)
    share(0)
    spread_tokens(1)
    for i in range(2):
        loop(0, NZ, lambda k: w_load(i, k).wait())
        loop(0, NZ, lambda k: w_get(i, k).wait_recv())
    select(0)
    stage(0, 0)
    stage(0, 1)
    share(1)
    spread_tokens(2)
    select(1)
    stage(1, 0)
    stage(0, 2)
    stage(1, 1)
    share(2)
    spread_tokens(3)
    stage(0, 3)
    select(2)
    stage(1, 2)
    share(3)
    loop(0, NZ, lambda k: w_load(2, k).wait())
    loop(0, NZ, lambda k: w_get(2, k).wait_recv())
    stage(0, 4)
    stage(2, 0)
    stage(1, 3)
    select(3)
    for t in range(1, 4):
        stage(0, 4 + t)
        stage(2, t)
        stage(1, 3 + t)
        stage(3, t - 1)
    stage(0, 8)
    stage(2, 4)
    stage(1, 7)
    stage(3, 3)
    spread(0)
    stage(2, 5)
    stage(1, 8)
    stage(3, 4)
    spread(1)
    collect(0)
    for s in range(2, far):
        ag_pass(2, s, closing=s == far - 1)
        ag_pass(3, s - 1)
        ag_down(2, s)
        ag_down(3, s - 1)
        if s == 2:
            collect(1)
    ag_last(2)
    ag_pass(3, far - 1, closing=True)
    ag_down(3, far - 1)
    spread(2)
    ag_last(3)
    spread(3)
    collect(2)
    collect(3)
    load[0, 0] = jnp.max(functools.reduce(jnp.maximum, loads)).astype(jnp.int32)

    def b_from(src):
        return remote(
            zout.at[0, 0], zback.at[src], b_send.at[0, 0], b_recv.at[src], (wide, src)
        )

    loop(1, NZ, lambda k: b_from(zs(k)).wait_recv())
    line = []
    for n in range(NZ):
        got = zback[n].astype(F32)
        line += [got[:8, :], got[8:, : block - WIDE_LO]]
    out[...] = jnp.concatenate(line, axis=1).astype(BF16)

    loop(1, NZ, lambda k: z_copy(zs(k)).wait_send())
    for i in range(3):
        loop(0, NZ, lambda k: w_give(i, k).wait_send())
    for h in range(GROUPS):
        loop(1, NX * NY, lambda k: g_copy(h, k).wait_send())
        m_copy(h, cc).wait_send()
        cm_copy(h, 1 - cc).wait_send()
        loop(1, NX * NY, lambda k: r_copy(h, k).wait_send())
        for j in range(2):
            pl.when(z != 2 * h + j)(lambda j=j: b_copy(h, j).wait_send())

    for h in range(GROUPS):
        for d in range(2):
            for s in range(far):
                for p in range(PIECES):
                    if s > 0 or halfway(d, p):
                        rs_sent(h, d, s, p)
                    if s < far - 1 or halfway(d, p):
                        ag_copy(h, d, s, p, z).wait_send()


class Copies:
    def __init__(self, send, recv):
        self.send, self.recv = send, recv
        self.used = 0
        self.started = []

    def slot(self):
        self.used += 1
        return self.used - 1

    def make(self, slot, src, dst, device):
        return pltpu.make_async_remote_copy(
            src_ref=src,
            dst_ref=dst,
            send_sem=self.send.at[slot],
            recv_sem=self.recv.at[slot],
            device_id=device,
            device_id_type=pl.DeviceIdType.MESH,
        )

    def go(self, slot, src, dst, device):
        copy = self.make(slot, src, dst, device)
        copy.start()
        self.started.append(copy)


def every_slot_kernel(
    tok,
    wg_hbm,
    wu_hbm,
    wd_hbm,
    out,
    zin,
    g,
    x,
    sel,
    wcol,
    wg,
    wu,
    wd,
    first,
    part,
    hid,
    acc,
    c,
    core_in,
    ra1,
    ra2,
    rb1,
    rb2,
    zout,
    zback,
    load_sem,
    send,
    recv,
    rs_send,
    rs_recv,
    ag_send,
    ag_recv,
):
    wide, z = lax.axis_index("wide"), lax.axis_index("narrow")
    cc = lax.rem(wide, NC)
    yy = lax.rem(wide // NC, NY)
    xx = wide // (NC * NY)
    block = x.shape[1]
    rows = x.shape[0]
    half = rows // 2
    sub = half // SUBS
    cols = wg.shape[1] // NZ

    def at(px, py, pc):
        return (px * NY + py) * NC + pc

    def xs(k):
        return lax.rem(xx + k, NX)

    def ys(k):
        return lax.rem(yy + k, NY)

    def zs(k):
        return lax.rem(z + k, NZ)

    xdev = {1: (at(xs(1), yy, cc), z), -1: (at(xs(3), yy, cc), z)}
    ydev = {1: (at(xx, ys(1), cc), z), -1: (at(xx, ys(3), cc), z)}
    mate = (at(xx, yy, 1 - cc), z)

    loads = [
        pltpu.make_async_copy(a, b, load_sem.at[i])
        for i, (a, b) in enumerate(((wg_hbm, wg), (wu_hbm, wu), (wd_hbm, wd)))
    ]
    for load in loads:
        load.start()

    barrier = pltpu.get_barrier_semaphore()
    peers = [xdev[1], xdev[-1], ydev[1], ydev[-1], mate] + [(wide, zs(k)) for k in range(1, NZ)]
    for peer in peers:
        pl.semaphore_signal(barrier, inc=1, device_id=peer, device_id_type=pl.DeviceIdType.MESH)
    pl.semaphore_wait(barrier, len(peers))

    copies = Copies(send, recv)

    zslots = {}
    for k in range(1, NZ):
        zslots[k] = copies.slot()
        copies.go(zslots[k], tok.at[zs(k)], zin.at[z], (wide, zs(k)))
    zin[z] = tok[z]
    for k in range(1, NZ):
        src = zs(NZ - k)
        copies.make(zslots[k], tok.at[src], zin.at[src], (wide, src)).wait_recv()
    arrived = zin[...].astype(F32)
    tokens_z = arrived.shape[0] * arrived.shape[1] // 2
    g[xx, yy, cc, :, :WIDE_LO] = arrived[:, :8, :].reshape(tokens_z, WIDE_LO).astype(BF16)
    g[xx, yy, cc, :, WIDE_LO:] = arrived[:, 8:, :].reshape(tokens_z, WIDE_LO).astype(BF16)

    def lane_a(pos):
        return lambda lo, n: g.at[pos, yy, cc, pl.ds(lo, n)]

    def lane_b(pos):
        return lambda lo, n: g.at[xx, pos, cc, pl.ds(32 + lo, n)]

    def plane_a(pos):
        return lambda lo, n: g.at[:, pos, cc, pl.ds(lo, n)]

    def plane_b(pos):
        return lambda lo, n: g.at[pos, :, cc, pl.ds(32 + lo, n)]

    def gather_start(region, step, dev):
        right, left = copies.slot(), copies.slot()
        own = region(step(0))(0, 32)
        copies.go(right, own, own, dev[1])
        copies.go(left, own, own, dev[-1])
        return right, left

    def gather_forward(region, step, dev, slots):
        right, left = copies.slot(), copies.slot()
        before, after = region(step(3)), region(step(1))
        copies.make(slots[0], before(0, 32), before(0, 32), dev[-1]).wait_recv()
        copies.go(right, before(0, 16), before(0, 16), dev[1])
        copies.make(slots[1], after(0, 32), after(0, 32), dev[1]).wait_recv()
        copies.go(left, after(16, 16), after(16, 16), dev[-1])
        return right, left

    def gather_end(region, step, dev, slots):
        far = region(step(2))
        copies.make(slots[0], far(0, 16), far(0, 16), dev[-1]).wait_recv()
        copies.make(slots[1], far(16, 16), far(16, 16), dev[1]).wait_recv()

    core_waits = []

    def to_mate(region, step, k):
        slot = copies.slot()
        copies.go(slot, region(step(k))(0, 32), region(step(k))(0, 32), mate)
        core_waits.append((slot, region, step, k))

    a1 = gather_start(lane_a, xs, xdev)
    b1 = gather_start(lane_b, ys, ydev)
    a2 = gather_forward(lane_a, xs, xdev, a1)
    b2 = gather_forward(lane_b, ys, ydev, b1)
    gather_end(lane_a, xs, xdev, a2)
    a3 = gather_start(plane_a, ys, ydev)
    gather_end(lane_b, ys, ydev, b2)
    b3 = gather_start(plane_b, xs, xdev)
    to_mate(plane_a, ys, 0)
    to_mate(plane_b, xs, 0)
    a4 = gather_forward(plane_a, ys, ydev, a3)
    b4 = gather_forward(plane_b, xs, xdev, b3)
    for k in (1, 3):
        to_mate(plane_a, ys, k)
        to_mate(plane_b, xs, k)
    gather_end(plane_a, ys, ydev, a4)
    to_mate(plane_a, ys, 2)
    gather_end(plane_b, xs, xdev, b4)
    to_mate(plane_b, xs, 2)
    other = {
        plane_a: lambda pos: g.at[:, pos, 1 - cc, pl.ds(0, 32)],
        plane_b: lambda pos: g.at[pos, :, 1 - cc, pl.ds(32, 32)],
    }
    for slot, region, step, k in core_waits:
        there = other[region](step(k))
        copies.make(slot, there, there, mate).wait_recv()

    batches = 8
    toks = NX * NY * NC * 64 // batches
    slots = rows // batches
    devs = slots // 4
    lane = lax.broadcasted_iota(jnp.int32, (toks, SIDE), 1)
    row = lax.broadcasted_iota(jnp.int32, (toks, SIDE), 0)
    mine = (lax.rem(lane, 32) == wide) & (lane < 96)
    square_r = lax.broadcasted_iota(jnp.int32, (toks, toks), 0)
    square_c = lax.broadcasted_iota(jnp.int32, (toks, toks), 1)
    lower = ((square_r // 8 == square_c // 8) & (square_c < square_r)).astype(F32).astype(BF16)
    for b in range(batches):
        here = g[b // 2, 2 * (b % 2) : 2 * (b % 2) + 2].reshape(toks, block + SIDE)
        weight = jnp.sum(
            jnp.where(mine, here[:, block:].astype(F32), 0.0), axis=1, keepdims=True
        )
        weight = jnp.broadcast_to(weight, (toks, SIDE))
        chosen = jnp.where(weight > 0.0, 1.0, 0.0)
        rank = dot(lower, chosen.astype(BF16)).astype(jnp.int32)
        place = rank * devs + row // 8
        pick = jnp.where((lane == place) & (weight > 0.0), 1.0, 0.0).astype(BF16)
        sel[b] = pick
        wcol[b] = weight
        taken = lax.dot_general(
            pick, here[:, :block], (((0,), (0,)), ((), ())), preferred_element_type=F32
        )
        x[b * slots : (b + 1) * slots, :] = taken.astype(BF16)

    loads[0].wait()
    loads[1].wait()
    zdev = ((wide, zs(1)), (wide, zs(NZ - 1)))

    def ring(s, d):
        return lax.rem(z + NZ - s, NZ) if d == 0 else lax.rem(z + s, NZ)

    def product(d, q, chunk):
        rows_here = x[pl.ds(pl.multiple_of(d * half + q * sub, sub), sub), :]
        at_cols = pl.ds(pl.multiple_of(chunk * cols, cols), cols)
        return dot(rows_here, wg[:, at_cols]), dot(rows_here, wu[:, at_cols])

    def rs_copy(d, s, q, src):
        return pltpu.make_async_remote_copy(
            src_ref=src,
            dst_ref=part.at[d, s, q],
            send_sem=rs_send.at[d, s, q],
            recv_sem=rs_recv.at[d, s, q],
            device_id=zdev[d],
            device_id_type=pl.DeviceIdType.MESH,
        )

    def ag_copy(d, s, q, chunk):
        here = hid.at[chunk, pl.ds(pl.multiple_of(d * half + q * sub, sub), sub)]
        return pltpu.make_async_remote_copy(
            src_ref=here,
            dst_ref=here,
            send_sem=ag_send.at[d, s, q],
            recv_sem=ag_recv.at[d, s, q],
            device_id=zdev[d],
            device_id_type=pl.DeviceIdType.MESH,
        )

    def each_sub(body):
        def step(q, carry):
            for d in range(2):
                body(d, q)
            return carry

        lax.fori_loop(0, SUBS, step, 0)

    def rs_first(d, q):
        gate, up = product(d, q, ring(1, d))
        first[d, q, :, :cols] = gate.astype(BF16)
        first[d, q, :, cols:] = up.astype(BF16)
        rs_copy(d, 0, q, first.at[d, q]).start()

    each_sub(rs_first)

    def rs_step(s, carry):
        def body(d, q):
            gate, up = product(d, q, ring(s + 1, d))
            rs_copy(d, s - 1, q, first.at[d, q]).wait_recv()
            here = part.at[d, s - 1, q]
            here[:, :cols] = (here[:, :cols].astype(F32) + gate).astype(BF16)
            here[:, cols:] = (here[:, cols:].astype(F32) + up).astype(BF16)
            rs_copy(d, s, q, here).start()

        each_sub(body)
        return carry

    lax.fori_loop(1, NZ - 1, rs_step, 0)
    loads[2].wait()

    def down(d, q, chunk):
        at_rows = pl.ds(pl.multiple_of(d * half + q * sub, sub), sub)
        at_cols = pl.ds(pl.multiple_of(chunk * cols, cols), cols)
        return at_rows, dot(hid[chunk, at_rows, :], wd[at_cols, :])

    def rs_last(d, q):
        gate, up = product(d, q, z)
        rs_copy(d, NZ - 2, q, first.at[d, q]).wait_recv()
        here = part.at[d, NZ - 2, q]
        gate = gate + here[:, :cols].astype(F32)
        up = up + here[:, cols:].astype(F32)
        hidden = gate / (1.0 + jnp.exp(-gate)) * up
        at_rows = pl.ds(pl.multiple_of(d * half + q * sub, sub), sub)
        hid[z, at_rows, :] = hidden.astype(BF16)
        ag_copy(d, 0, q, z).start()
        at_rows, value = down(d, q, z)
        acc[at_rows, :] = value

    each_sub(rs_last)

    def ag_step(s, carry):
        def body(d, q):
            chunk = ring(s, d)
            ag_copy(d, s - 1, q, chunk).wait_recv()
            ag_copy(d, s, q, chunk).start()
            at_rows, value = down(d, q, chunk)
            acc[at_rows, :] = acc[at_rows, :] + value

        each_sub(body)
        return carry

    lax.fori_loop(1, NZ - 1, ag_step, 0)

    core_slots = [copies.slot() for _ in range(NX)]
    for b in range(batches):
        d, q = b // SUBS, b % SUBS
        chunk = ring(NZ - 1, d)
        ag_copy(d, NZ - 2, q, chunk).wait_recv()
        at_rows, value = down(d, q, chunk)
        expert_out = (acc[at_rows, :] + value).astype(BF16)
        mixed = dot(sel[b], expert_out) * wcol[b][:, :1]
        c[b // 2, 2 * (b % 2) : 2 * (b % 2) + 2] = mixed.astype(BF16).reshape(2, NC, 64, block)
        if b % 2 == 1:
            copies.go(core_slots[b // 2], c.at[b // 2, :, 1 - cc], core_in.at[b // 2], mate)
    for px in range(NX):
        copies.make(core_slots[px], c.at[px, :, cc], core_in.at[px], mate).wait_recv()
        c[px, :, cc] = (c[px, :, cc].astype(F32) + core_in[px].astype(F32)).astype(BF16)

    def c_plane_a(pos, lo, n):
        return c.at[:, pos, cc, pl.ds(lo, n)]

    def c_plane_b(pos, lo, n):
        return c.at[pos, :, cc, pl.ds(32 + lo, n)]

    def c_lane_a(pos, lo, n):
        return c.at[pos, yy, cc, pl.ds(lo, n)]

    def c_lane_b(pos, lo, n):
        return c.at[xx, pos, cc, pl.ds(32 + lo, n)]

    def add_into(ref, other_ref):
        ref[...] = (ref[...].astype(F32) + other_ref[...].astype(F32)).astype(BF16)

    def scatter_start(region, step, dev, buf):
        right, left = copies.slot(), copies.slot()
        copies.go(right, region(step(2), 0, 16), buf.at[0], dev[1])
        copies.go(left, region(step(2), 16, 16), buf.at[1], dev[-1])
        return right, left

    def scatter_forward(region, step, dev, buf, buf2, slots):
        right, left = copies.slot(), copies.slot()
        copies.make(slots[0], region(step(2), 0, 16), buf.at[0], dev[-1]).wait_recv()
        add_into(region(step(1), 0, 16), buf.at[0])
        copies.go(right, region(step(1), 0, 32), buf2.at[0], dev[1])
        copies.make(slots[1], region(step(2), 16, 16), buf.at[1], dev[1]).wait_recv()
        add_into(region(step(3), 16, 16), buf.at[1])
        copies.go(left, region(step(3), 0, 32), buf2.at[1], dev[-1])
        return right, left

    def scatter_end(region, step, dev, buf2, slots):
        copies.make(slots[0], region(step(0), 0, 32), buf2.at[0], dev[-1]).wait_recv()
        copies.make(slots[1], region(step(0), 0, 32), buf2.at[1], dev[1]).wait_recv()
        here = region(step(0), 0, 32)
        return here[...].astype(F32) + buf2[0].astype(F32) + buf2[1].astype(F32)

    a1 = scatter_start(c_plane_a, ys, ydev, ra1.at[0])
    b1 = scatter_start(c_plane_b, xs, xdev, ra1.at[1])
    a2 = scatter_forward(c_plane_a, ys, ydev, ra1.at[0], ra2.at[0], a1)
    b2 = scatter_forward(c_plane_b, xs, xdev, ra1.at[1], ra2.at[1], b1)
    total = scatter_end(c_plane_a, ys, ydev, ra2.at[0], a2)
    c[:, yy, cc, :32, :] = total.astype(BF16)
    a3 = scatter_start(c_lane_a, xs, xdev, rb1.at[0])
    total = scatter_end(c_plane_b, xs, xdev, ra2.at[1], b2)
    c[xx, :, cc, 32:, :] = total.astype(BF16)
    b3 = scatter_start(c_lane_b, ys, ydev, rb1.at[1])
    a4 = scatter_forward(c_lane_a, xs, xdev, rb1.at[0], rb2.at[0], a3)
    b4 = scatter_forward(c_lane_b, ys, ydev, rb1.at[1], rb2.at[1], b3)
    sums = [
        scatter_end(c_lane_a, xs, xdev, rb2.at[0], a4),
        scatter_end(c_lane_b, ys, ydev, rb2.at[1], b4),
    ]

    for i, total in enumerate(sums):
        lo = total[:, :WIDE_LO].reshape(4, 8, WIDE_LO)
        hi = total[:, WIDE_LO:].reshape(4, 8, block - WIDE_LO)
        hi = jnp.concatenate([hi, jnp.zeros((4, 8, 2 * WIDE_LO - block), F32)], axis=2)
        zout[4 * i : 4 * i + 4] = jnp.concatenate([lo, hi], axis=1).astype(BF16)
    zslots = {}
    for k in range(1, NZ):
        zslots[k] = copies.slot()
        copies.go(zslots[k], zout.at[zs(k)], zback.at[z], (wide, zs(k)))
    zback[z] = zout[z]
    for k in range(1, NZ):
        src = zs(NZ - k)
        copies.make(zslots[k], zout.at[src], zback.at[src], (wide, src)).wait_recv()
    pieces = []
    for n in range(NZ):
        got = zback[n].astype(F32)
        pieces += [got[:8, :], got[8:, : block - WIDE_LO]]
    out[...] = jnp.concatenate(pieces, axis=1).astype(BF16)

    for copy in copies.started:
        copy.wait_send()

    def drain(s, carry):
        def body(d, q):
            rs_copy(d, s, q, first.at[d, q]).wait_send()
            ag_copy(d, s, q, ring(s, d)).wait_send()

        each_sub(body)
        return carry

    lax.fori_loop(0, NZ - 1, drain, 0)


def every_slot(tok_rows, width, capacity, tok, w_gate, w_up, w_down):
    block, ff = w_gate.shape
    rows = NX * NY * NC * NZ * 2 * capacity
    half = rows // 2
    sub = half // SUBS
    cols = ff // NZ
    vmem = pl.BlockSpec(memory_space=pltpu.VMEM)
    hbm = pl.BlockSpec(memory_space=pl.ANY)
    line = block + SIDE
    copies = 7 + 24 + 4 + 16 + 7
    return pl.pallas_call(
        every_slot_kernel,
        out_shape=jax.ShapeDtypeStruct((tok_rows, width), BF16),
        in_specs=[vmem, hbm, hbm, hbm],
        out_specs=vmem,
        scratch_shapes=[
            pltpu.VMEM((NZ, 16, WIDE_LO), BF16),
            pltpu.VMEM((NX, NY, NC, 64, line), BF16),
            pltpu.VMEM((rows, block), BF16),
            pltpu.VMEM((8, 256, SIDE), BF16),
            pltpu.VMEM((8, 256, SIDE), F32),
            pltpu.VMEM((block, ff), BF16),
            pltpu.VMEM((block, ff), BF16),
            pltpu.VMEM((ff, block), BF16),
            pltpu.VMEM((2, SUBS, sub, 2 * cols), BF16),
            pltpu.VMEM((2, NZ - 1, SUBS, sub, 2 * cols), BF16),
            pltpu.VMEM((NZ, rows, cols), BF16),
            pltpu.VMEM((rows, block), F32),
            pltpu.VMEM((NX, NY, NC, 64, block), BF16),
            pltpu.VMEM((NX, NY, 64, block), BF16),
            pltpu.VMEM((2, 2, 4, 16, block), BF16),
            pltpu.VMEM((2, 2, 4, 32, block), BF16),
            pltpu.VMEM((2, 2, 16, block), BF16),
            pltpu.VMEM((2, 2, 32, block), BF16),
            pltpu.VMEM((NZ, 16, WIDE_LO), BF16),
            pltpu.VMEM((NZ, 16, WIDE_LO), BF16),
            pltpu.SemaphoreType.DMA((3,)),
            pltpu.SemaphoreType.DMA((copies,)),
            pltpu.SemaphoreType.DMA((copies,)),
            pltpu.SemaphoreType.DMA((2, NZ - 1, SUBS)),
            pltpu.SemaphoreType.DMA((2, NZ - 1, SUBS)),
            pltpu.SemaphoreType.DMA((2, NZ - 1, SUBS)),
            pltpu.SemaphoreType.DMA((2, NZ - 1, SUBS)),
        ],
        compiler_params=pltpu.CompilerParams(
            collective_id=1, has_side_effects=True, vmem_limit_bytes=58 * 1024 * 1024
        ),
        cost_estimate=pl.CostEstimate(
            flops=6 * rows * block * ff, bytes_accessed=6 * block * ff, transcendentals=rows * cols
        ),
        name="every_slot",
    )(tok, w_gate, w_up, w_down)


def on_device(tokens, routes, gates, fallback, w_gate, w_up, w_down):
    experts = lax.axis_size("wide")
    tok_rows, width = tokens.shape
    capacity = min(tok_rows // 2, tok_rows * routes.shape[1] // experts)
    weights = (w_gate[0], w_up[0], w_down[0])
    mixed, tok, load = packed(capacity, tokens, routes, gates, fallback[None, :], *weights)
    return lax.cond(
        load[0, 0] > ROWS,
        lambda: every_slot(tok_rows, width, capacity, tok, *weights),
        lambda: mixed,
    )


def packed(capacity, tokens, routes, gates, fallback, w_gate, w_up, w_down):
    block, ff = w_gate.shape
    tok_rows, width = tokens.shape
    cols = ff // NC // NZ
    vmem = pl.BlockSpec(memory_space=pltpu.VMEM)
    hbm = pl.BlockSpec(memory_space=pl.ANY)
    line = block + SIDE
    dma = pltpu.SemaphoreType.DMA
    half = BOUNDS[PIECES // 2]
    return pl.pallas_call(
        functools.partial(kernel, capacity),
        out_shape=(
            jax.ShapeDtypeStruct((tok_rows, width), BF16),
            jax.ShapeDtypeStruct((NZ, 16, WIDE_LO), BF16),
            jax.ShapeDtypeStruct((1, 1), jnp.int32),
        ),
        in_specs=[vmem] * 4 + [hbm] * 3,
        out_specs=(vmem, vmem, pl.BlockSpec(memory_space=pltpu.SMEM)),
        scratch_shapes=[
            pltpu.VMEM((NZ, 16, WIDE_LO), BF16),
            pltpu.VMEM((NX, NY, NC, 64, line), BF16),
            pltpu.VMEM((GROUPS, ROWS, 2 * block), BF16),
            pltpu.VMEM((GROUPS, 512, ROWS), BF16),
            pltpu.VMEM((GROUPS, ROWS, SIDE), F32),
            pltpu.VMEM((GROUPS, ROWS, SIDE), BF16),
            pltpu.VMEM((NZ, 2 * block, 2 * cols), BF16),
            pltpu.VMEM((NZ, 2 * cols, block), BF16),
            pltpu.VMEM((GROUPS, 2, half, 2 * cols), BF16),
            pltpu.VMEM((GROUPS, 2, NZ // 2, ROWS, 2 * cols), BF16),
            pltpu.VMEM((NZ, GROUPS, ROWS, cols), BF16),
            pltpu.VMEM((2, ROWS, block), F32),
            pltpu.VMEM((GROUPS, NX, NY, NC, 16, block), BF16),
            pltpu.VMEM((GROUPS, NX, NY, 16, block), BF16),
            pltpu.VMEM((GROUPS, NX, NY, 16, block), BF16),
            pltpu.VMEM((GROUPS, 2, 16, WIDE_LO), BF16),
            pltpu.VMEM((NZ, 16, WIDE_LO), BF16),
            dma((3, NZ)),
            dma((3, NZ)),
            dma((3, NZ)),
            dma((NZ,)),
            dma((NZ,)),
            dma((GROUPS, NX * NY)),
            dma((GROUPS, NX * NY)),
            dma((GROUPS,)),
            dma((GROUPS,)),
            dma((GROUPS, 2, NZ // 2, PIECES)),
            dma((GROUPS, 2, NZ // 2, PIECES)),
            dma((GROUPS, 2, NZ // 2, PIECES)),
            dma((GROUPS, 2, NZ // 2, PIECES)),
            dma((GROUPS,)),
            dma((GROUPS,)),
            dma((GROUPS, NX * NY)),
            dma((GROUPS, NX * NY)),
            dma((GROUPS, 2)),
            dma((NZ,)),
        ],
        compiler_params=pltpu.CompilerParams(
            collective_id=0, has_side_effects=True, vmem_limit_bytes=60 * 1024 * 1024
        ),
        cost_estimate=pl.CostEstimate(
            flops=6 * GROUPS * ROWS * block * ff,
            bytes_accessed=6 * block * ff,
            transcendentals=GROUPS * ROWS * cols,
        ),
        name="packed",
    )(tokens, routes, gates, fallback, w_gate, w_up, w_down)


def solution(mesh):
    placed = (
        P(("wide", "narrow"), None),
        P(("wide", "narrow"), None),
        P(("wide", "narrow"), None),
        P(),
        P("wide", "narrow", None),
        P("wide", "narrow", None),
        P("wide", None, "narrow"),
    )
    return jax.shard_map(
        on_device,
        mesh=mesh,
        in_specs=placed,
        out_specs=P(("wide", "narrow"), None),
        check_vma=False,
    )
```
